256 devices in a mesh: prefix: 16 (over y, z_lo), resp: 16 (over z_hi, x, core).
Axes of the slice: x: 4, y: 4, z: 8 (z_hi: 2, z_lo: 4; z = z_hi * 4 + z_lo), core: 2. Of those that a mesh axis runs over, the one named last changes fastest.
Arguments:
- response_queries: bfloat16 [16, 2048, 2560], P('resp', 'prefix'), may hold values from -120 to 120
- response_keys: bfloat16 [16, 2048, 512], P('resp', 'prefix'), may hold values from -6 to 6
- response_values: bfloat16 [16, 2048, 512], P('resp', 'prefix'), may hold values from -6 to 6
- prompt_keys: bfloat16 [768, 512], P('prefix'), may hold values from -6.1 to 6.1
- prompt_values: bfloat16 [768, 512], P('prefix'), may hold values from -6 to 6
- output_grad: bfloat16 [16, 2048, 2560], P('resp', 'prefix'), may hold values from -6 to 6
- lengths: int32 [16], replicated, may hold values from 1 to 2048, 17408 in all
Outputs:
- attention_out: bfloat16 [16, 2048, 2560], P('resp', 'prefix')
- query_grad: bfloat16 [16, 2048, 2560], P('resp', 'prefix')
- response_key_grad: float32 [16, 2048, 512], P('resp', 'prefix')
- response_value_grad: float32 [16, 2048, 512], P('resp', 'prefix')
- prompt_key_grad: float32 [768, 512], P('prefix')
- prompt_value_grad: float32 [768, 512], P('prefix')
The draws below stay inside these ranges and needn't reach their ends.
Inputs may be any that keep to these rules, and one draw needn't show every extreme that they name: `lengths`: the longest response has exactly 2048 positions.
All inputs are finite; a program needn't handle non-finite values.
Results may differ from the reference program's by a relative error of at most 0.035.
Values may be sent and summed in bfloat16 or wider, within the bound.
No kernel may reach another device: no remote copies, remote signals or barrier semaphores. Data moves between devices by JAX's collectives and lax.ppermute only.
A program may use at most 128 MiB of HBM per device.

```python
import math
import jax
import jax.numpy as jnp
import numpy as np
from jax import lax

H = 20
G = 4
HD = 128
RL = 2048
P_SIZE = 768
NRESP = 16


def base_keys(key):
    return jnp.clip(jax.random.normal(key, (P_SIZE, G * HD), jnp.float32), -6.0, 6.0)


def draw_prompt_keys(key, part):
    keys_drawn = base_keys(key)
    return keys_drawn.astype(jnp.bfloat16)


def draw_response_queries(key, part):
    key = jax.random.fold_in(key, 12)
    queries = jnp.clip(jax.random.normal(key, (NRESP, RL, H * HD), jnp.float32), -6.0, 6.0)
    return queries.astype(jnp.bfloat16)


def shard_levels(own_key, dims, shards, low, top_value):
    def one(position, blocks):
        heights = jax.random.uniform(jax.random.fold_in(jax.random.fold_in(own_key, 6), position), (blocks,), jnp.float32, low / len(shards), top_value / len(shards))
        return jnp.repeat(jnp.exp(heights), dims[position] // blocks).reshape((-1,) + (1,) * (len(dims) - position - 1))

    level = one(*shards[0])
    for cut in shards[1:]:
        level = level * one(*cut)
    return level


def split_up(number_of, total, limit, lean):
    loads = [(1 << 20) // math.isqrt(standing ** lean) + 1 for standing in range(2, number_of + 1)]
    rest, holding = total - limit - (number_of - 1), [1] * (number_of - 1)
    while rest > 0:
        movable = [i for i in range(number_of - 1) if holding[i] < limit]
        pool, left = sum([loads[i] for i in movable]), rest
        for i in movable:
            addition = min(limit - holding[i], max(1, left * loads[i] // pool), rest)
            holding[i] = holding[i] + addition
            rest = rest - addition
    return np.array([limit] + holding)


def uneven_parts(key, amount, total, bound, slope):
    if amount == 2:
        one = jax.random.randint(key, (), max(1, total - bound), min(bound, total - 1) + 1)
        return jnp.stack([one, total - one])
    sizes = jnp.asarray(split_up(amount, total, bound, slope), jnp.int32)
    twos = (amount - 1) // 2
    giver, receiver = sizes[1:1 + 2 * twos:2], sizes[2:2 + 2 * twos:2]
    slack = jnp.minimum(giver - 1, bound - receiver)
    moved = jax.random.randint(jax.random.fold_in(key, 1), (twos,), 0, 1 << 20) % (slack + 1)
    sizes = sizes.at[1:1 + 2 * twos:2].set(giver - moved).at[2:2 + 2 * twos:2].set(receiver + moved)
    return sizes[jax.random.permutation(jax.random.fold_in(key, 2), amount)]


def gaussian(rng, dims, deviation, limit, shards=(), kind=jnp.bfloat16):
    gain = shard_levels(rng, dims, shards, -0.22, 0.18) if shards else 1.0
    values = jax.random.normal(rng, dims, jnp.float32) * deviation * gain
    return jnp.minimum(jnp.maximum(values, -limit), limit).astype(kind)


def setup_inputs(seed: int = 0) -> dict:
    key_of = jax.random.split(jax.random.key(seed), 8)
    response_queries = draw_response_queries(jax.random.fold_in(key_of[7], 71), 0)
    response_keys = gaussian(key_of[1], (NRESP, RL, G * HD), 1.0, 6.0, ((0, 16), (1, 16)))
    response_values = gaussian(key_of[2], (NRESP, RL, G * HD), 1.0, 6.0, ((0, 16), (1, 16)))
    prompt_keys = draw_prompt_keys(jax.random.fold_in(key_of[7], 71), 0)
    prompt_values = gaussian(key_of[4], (P_SIZE, G * HD), 1.0, 6.0, ((0, 16),))
    output_grad = gaussian(key_of[5], (NRESP, RL, H * HD), 1.0, 6.0, ((0, 16), (1, 16)))
    lengths = uneven_parts(key_of[6], NRESP, NRESP * RL // 2 + RL // 2, RL, 2).astype(jnp.int32)
    return {"response_queries": response_queries, "response_keys": response_keys, "response_values": response_values, "prompt_keys": prompt_keys, "prompt_values": prompt_values, "output_grad": output_grad, "lengths": lengths}


MASKED = -1e+30

def response_terms(queries, key_rows, value_rows, grad_rows, row_valid, key_live, scaling):
    scores = jnp.einsum('tjd,kd->jtk', queries.astype(jnp.float32), key_rows.astype(jnp.float32)) * scaling
    scores = jnp.where(key_live[None], scores, MASKED)
    maximum = lax.optimization_barrier(jnp.max(scores, axis=-1, keepdims=True))
    log_norm = maximum + jnp.log(lax.optimization_barrier(jnp.sum(jnp.exp(scores - maximum), axis=-1, keepdims=True)))
    attend = jnp.exp(scores - log_norm)
    attend_low = attend.astype(jnp.bfloat16)
    attention = jnp.einsum('jtk,kd->tjd', attend_low.astype(jnp.float32), value_rows.astype(jnp.float32))
    attention = jnp.where(row_valid[:, None, None], attention, 0.0).astype(jnp.bfloat16)
    row_delta = lax.optimization_barrier(jnp.sum(grad_rows.astype(jnp.float32) * attention.astype(jnp.float32), axis=-1)).T
    grad_attend = jnp.einsum('tjd,kd->jtk', grad_rows.astype(jnp.float32), value_rows.astype(jnp.float32))
    grad_scores = (attend * (grad_attend - row_delta[..., None])).astype(jnp.bfloat16)
    query_grad = (jnp.einsum('jtk,kd->tjd', grad_scores.astype(jnp.float32), key_rows.astype(jnp.float32)) * scaling).astype(jnp.bfloat16)
    key_grad = jnp.einsum('jtk,tjd->kd', grad_scores.astype(jnp.float32), queries.astype(jnp.float32)) * scaling
    value_grad = jnp.einsum('jtk,tjd->kd', attend_low.astype(jnp.float32), grad_rows.astype(jnp.float32))
    return (attention, query_grad, key_grad, value_grad)

def reference(response_queries, response_keys, response_values, prompt_keys, prompt_values, output_grad, lengths):
    scaling = 1.0 / math.sqrt(HD)
    per_group = H // G
    positions = jnp.arange(RL, dtype=jnp.int32)
    key_index = jnp.arange(P_SIZE + RL, dtype=jnp.int32)
    own_index = key_index - P_SIZE
    prompt_key_heads = prompt_keys.reshape(P_SIZE, G, HD).transpose(1, 0, 2)
    prompt_value_heads = prompt_values.reshape(P_SIZE, G, HD).transpose(1, 0, 2)

    def one_response(running, sliced):
        queries, key_block, value_block, grad_block, resp_length = sliced
        row_valid = positions < resp_length
        grad_block = jnp.where(row_valid[:, None], grad_block, jnp.zeros_like(grad_block))
        key_live = (key_index[None, :] < P_SIZE) | (own_index[None, :] <= positions[:, None]) & (own_index[None, :] < resp_length)
        query_heads = queries.reshape(RL, G, per_group, HD).transpose(1, 0, 2, 3)
        grad_heads = grad_block.reshape(RL, G, per_group, HD).transpose(1, 0, 2, 3)
        key_heads = jnp.concatenate([prompt_key_heads, key_block.reshape(RL, G, HD).transpose(1, 0, 2)], axis=1)
        value_heads = jnp.concatenate([prompt_value_heads, value_block.reshape(RL, G, HD).transpose(1, 0, 2)], axis=1)

        def group_terms(group_args):
            return response_terms(group_args[0], group_args[1], group_args[2], group_args[3], row_valid, key_live, scaling)
        attention, query_grad, key_grad, value_grad = lax.map(group_terms, (query_heads, key_heads, value_heads, grad_heads))
        attention = attention.transpose(1, 0, 2, 3).reshape(RL, H * HD)
        query_grad = query_grad.transpose(1, 0, 2, 3).reshape(RL, H * HD)
        prompt_key_sum, prompt_value_sum = running
        prompt_key_sum = prompt_key_sum + key_grad[:, :P_SIZE]
        prompt_value_sum = prompt_value_sum + value_grad[:, :P_SIZE]
        resp_key_grad = key_grad[:, P_SIZE:].transpose(1, 0, 2).reshape(RL, G * HD)
        resp_value_grad = value_grad[:, P_SIZE:].transpose(1, 0, 2).reshape(RL, G * HD)
        return ((prompt_key_sum, prompt_value_sum), (attention, query_grad, resp_key_grad, resp_value_grad))
    zeros = jnp.zeros((G, P_SIZE, HD), jnp.float32)
    sums, stacked = lax.scan(one_response, (zeros, zeros), (response_queries, response_keys, response_values, output_grad, lengths))
    prompt_key_grad = sums[0].transpose(1, 0, 2).reshape(P_SIZE, G * HD)
    prompt_value_grad = sums[1].transpose(1, 0, 2).reshape(P_SIZE, G * HD)
    return (stacked[0], stacked[1], stacked[2], stacked[3], prompt_key_grad, prompt_value_grad)
```

```python
import math

import jax
import jax.numpy as jnp
from jax import lax
from jax.experimental import pallas as pl
from jax.experimental.pallas import tpu as pltpu
from jax.sharding import PartitionSpec as P

HD = 128
BLOCK = 128
PROMPT_ROWS = 48
PIECE = PROMPT_ROWS + BLOCK
HEADS = 5
NY = 4
NZ = 4
PROMPT = PROMPT_ROWS * NY * NZ
KEYS = PROMPT + BLOCK * NY * NZ
ROWS = NY * HEADS * BLOCK
CHUNK = 256
TILE = 256
MASKED = -1e30
SCALE = 1.0 / math.sqrt(HD)
SCALE2 = SCALE * math.log2(math.e)
F32 = jnp.float32
BF16 = jnp.bfloat16
CLASSES = ((0, 2, 5, 3), (2, 5, 7, 3), (5, 7, 9, 7), (7, 10, 11, 7))


def attend_kernel(
    info,
    q0, q1, q2, q3,
    g0, g1, g2, g3,
    kv0, kv1, kv2, kv3,
    a0, a1, a2, a3,
    d0, d1, d2, d3,
    r0, r1, r2, r3,
    qs, gs, ks, vs, kt, vt, sc, pm, dk, dv, os, ds_out,
):
    y = info[0]
    z = info[1]
    length = info[2]
    for s, (q, g) in enumerate(((q0, g0), (q1, g1), (q2, g2), (q3, g3))):
        block = lax.rem(y - s + NY, NY)
        start = (block * NZ + z) * BLOCK
        valid = (lax.broadcasted_iota(jnp.int32, (BLOCK, HD), 0) + start) < length
        for j in range(HEADS):
            at = pl.ds(pl.multiple_of((block * HEADS + j) * BLOCK, BLOCK), BLOCK)
            cols = slice(j * HD, (j + 1) * HD)
            qs[at, :] = q[:, cols]
            gs[at, :] = jnp.where(valid, g[:, cols].astype(F32), 0.0).astype(BF16)
    for s, kv in enumerate((kv0, kv1, kv2, kv3)):
        zp = lax.rem(z - s + NZ, NZ)
        for b in range(NY):
            at = pl.ds(pl.multiple_of((zp * NY + b) * PROMPT_ROWS, PROMPT_ROWS), PROMPT_ROWS)
            ks[at, :] = kv[b, 0, :PROMPT_ROWS, :]
            vs[at, :] = kv[b, 1, :PROMPT_ROWS, :]
            at = pl.ds(pl.multiple_of(PROMPT + (b * NZ + zp) * BLOCK, BLOCK), BLOCK)
            ks[at, :] = kv[b, 0, PROMPT_ROWS:, :]
            vs[at, :] = kv[b, 1, PROMPT_ROWS:, :]
    for c in range(KEYS // BLOCK):
        rows = slice(c * BLOCK, (c + 1) * BLOCK)
        kt[:, rows] = ks[rows, :].T
        vt[:, rows] = vs[rows, :].T
    dk[...] = jnp.zeros_like(dk)
    dv[...] = jnp.zeros_like(dv)

    def tile_step(tile, chunks, first_masked):
        at = pl.ds(pl.multiple_of(tile * TILE, TILE), TILE)
        u = tile * 2
        block_lo = u // HEADS
        block_hi = (u + 1) // HEADS
        lane = lax.broadcasted_iota(jnp.int32, (1, TILE), 1)
        pos_lo = (block_lo * NZ + z) * BLOCK
        pos_hi = (block_hi * NZ + z) * BLOCK - BLOCK
        query_pos = lane + jnp.where(lane < BLOCK, pos_lo, pos_hi)

        @pl.when(pos_lo < length)
        def _():
            q = qs[at, :]
            qt = q.T
            top = jnp.full((8, TILE), MASKED, F32)
            for c in range(chunks):
                rows = slice(c * CHUNK, (c + 1) * CHUNK)
                s = jnp.dot(ks[rows, :], qt, preferred_element_type=F32)
                if c >= first_masked:
                    key_pos = lax.broadcasted_iota(jnp.int32, (CHUNK, TILE), 0) + (
                        c * CHUNK - PROMPT
                    )
                    s = jnp.where(key_pos <= query_pos, s, MASKED)
                sc[rows, :] = s
                top = jnp.maximum(top, jnp.max(s.reshape(CHUNK // 8, 8, TILE), axis=0))
            top = jnp.max(top, axis=0, keepdims=True)
            total = jnp.zeros((8, TILE), F32)
            out_t = jnp.zeros((HD, TILE), F32)
            for c in range(chunks):
                rows = slice(c * CHUNK, (c + 1) * CHUNK)
                p = jnp.exp2((sc[rows, :] - top) * SCALE2)
                total = total + jnp.sum(p.reshape(CHUNK // 8, 8, TILE), axis=0)
                low = p.astype(BF16)
                pm[rows, :] = low
                out_t = out_t + jnp.dot(vt[:, rows], low, preferred_element_type=F32)
            inv = 1.0 / jnp.sum(total, axis=0, keepdims=True)
            out_t = out_t * inv
            valid = query_pos < length
            os[at, :] = jnp.where(valid, out_t, 0.0).T.astype(BF16)
            grad_t = gs[at, :].astype(F32).T
            delta = jnp.sum(grad_t * out_t, axis=0, keepdims=True) * inv
            grad_t = grad_t * inv
            grad = grad_t.T.astype(BF16)
            grad_t = grad_t.astype(BF16)
            dq_t = jnp.zeros((HD, TILE), F32)
            for c in range(chunks):
                rows = slice(c * CHUNK, (c + 1) * CHUNK)
                dp = jnp.dot(vs[rows, :], grad_t, preferred_element_type=F32)
                low = pm[rows, :]
                ds = (low.astype(F32) * (dp - delta)).astype(BF16)
                dv[rows, :] += jnp.dot(low, grad, preferred_element_type=F32)
                dk[rows, :] += jnp.dot(ds, q, preferred_element_type=F32)
                dq_t = dq_t + jnp.dot(kt[:, rows], ds, preferred_element_type=F32)
            ds_out[at, :] = (dq_t * SCALE).T.astype(BF16)

        @pl.when(pos_lo >= length)
        def _():
            os[at, :] = jnp.zeros((TILE, HD), BF16)
            ds_out[at, :] = jnp.zeros((TILE, HD), BF16)

    for first, last, chunks, first_masked in CLASSES:

        def step(tile, carry, chunks=chunks, first_masked=first_masked):
            tile_step(tile, chunks, first_masked)
            return carry

        lax.fori_loop(first, last, step, 0)

    for s, (a, d) in enumerate(((a0, d0), (a1, d1), (a2, d2), (a3, d3))):
        block = lax.rem(y + s, NY)
        for j in range(HEADS):
            at = pl.ds(pl.multiple_of((block * HEADS + j) * BLOCK, BLOCK), BLOCK)
            cols = slice(j * HD, (j + 1) * HD)
            a[:, cols] = os[at, :]
            d[:, cols] = ds_out[at, :]
    for s, r in enumerate((r0, r1, r2, r3)):
        zp = lax.rem(z + s, NZ)
        for b in range(NY):
            at = pl.ds(pl.multiple_of((zp * NY + b) * PROMPT_ROWS, PROMPT_ROWS), PROMPT_ROWS)
            r[b, 0, :PROMPT_ROWS, :] = (dk[at, :] * SCALE).astype(BF16)
            r[b, 1, :PROMPT_ROWS, :] = dv[at, :].astype(BF16)
            at = pl.ds(pl.multiple_of(PROMPT + (b * NZ + zp) * BLOCK, BLOCK), BLOCK)
            r[b, 0, PROMPT_ROWS:, :] = (dk[at, :] * SCALE).astype(BF16)
            r[b, 1, PROMPT_ROWS:, :] = dv[at, :].astype(BF16)


def attend(info, queries, grads, keyvals):
    vmem = pl.BlockSpec(memory_space=pltpu.VMEM)
    row_piece = jax.ShapeDtypeStruct((BLOCK, HEADS * HD), BF16)
    key_piece = jax.ShapeDtypeStruct((NY, 2, PIECE, HD), BF16)
    return pl.pallas_call(
        attend_kernel,
        out_shape=[row_piece] * 8 + [key_piece] * 4,
        in_specs=[pl.BlockSpec(memory_space=pltpu.SMEM)] + [vmem] * 12,
        out_specs=[vmem] * 12,
        scratch_shapes=[
            pltpu.VMEM((ROWS, HD), BF16),
            pltpu.VMEM((ROWS, HD), BF16),
            pltpu.VMEM((KEYS, HD), BF16),
            pltpu.VMEM((KEYS, HD), BF16),
            pltpu.VMEM((HD, KEYS), BF16),
            pltpu.VMEM((HD, KEYS), BF16),
            pltpu.VMEM((KEYS, TILE), F32),
            pltpu.VMEM((KEYS, TILE), BF16),
            pltpu.VMEM((KEYS, HD), F32),
            pltpu.VMEM((KEYS, HD), F32),
            pltpu.VMEM((ROWS, HD), BF16),
            pltpu.VMEM((ROWS, HD), BF16),
        ],
        compiler_params=pltpu.CompilerParams(vmem_limit_bytes=48 * 2**20),
        name="attend",
    )(info, *queries, *grads, *keyvals)


def place_rows_kernel(info, a0, a1, a2, a3, d0, d1, d2, d3, a, d):
    y = info[0]
    for s, (ap, dp) in enumerate(((a0, d0), (a1, d1), (a2, d2), (a3, d3))):
        width = HEADS * HD
        at = pl.ds(pl.multiple_of(lax.rem(y - s + NY, NY) * width, width), width)
        a[:, at] = ap[...]
        d[:, at] = dp[...]


def place_rows(info, att, dq):
    vmem = pl.BlockSpec(memory_space=pltpu.VMEM)
    out = jax.ShapeDtypeStruct((BLOCK, NY * HEADS * HD), BF16)
    return pl.pallas_call(
        place_rows_kernel,
        out_shape=[out, out],
        in_specs=[pl.BlockSpec(memory_space=pltpu.SMEM)] + [vmem] * 8,
        out_specs=[vmem] * 2,
        name="place_rows",
    )(info, *att, *dq)


def place_keys_kernel(info, p0, p1, p2, p3, dk, dv, prompt):
    y = info[0]
    for s, p in enumerate((p0, p1, p2, p3)):
        at = pl.ds(pl.multiple_of(lax.rem(y - s + NY, NY) * HD, HD), HD)
        prompt[0, :, at] = p[0, :PROMPT_ROWS, :].astype(F32)
        prompt[1, :, at] = p[1, :PROMPT_ROWS, :].astype(F32)
        dk[:, at] = p[0, PROMPT_ROWS:, :].astype(F32)
        dv[:, at] = p[1, PROMPT_ROWS:, :].astype(F32)


def place_keys(info, pieces):
    vmem = pl.BlockSpec(memory_space=pltpu.VMEM)
    return pl.pallas_call(
        place_keys_kernel,
        out_shape=[
            jax.ShapeDtypeStruct((BLOCK, NY * HD), F32),
            jax.ShapeDtypeStruct((BLOCK, NY * HD), F32),
            jax.ShapeDtypeStruct((2, PROMPT_ROWS, NY * HD), F32),
        ],
        in_specs=[pl.BlockSpec(memory_space=pltpu.SMEM)] + [vmem] * 4,
        out_specs=[vmem] * 3,
        name="place_keys",
    )(info, *pieces)


def y_shift(a, s):
    pairs = [(i * NZ + k, (i + s) % NY * NZ + k) for i in range(NY) for k in range(NZ)]
    return lax.ppermute(a, "prefix", pairs)


def z_shift(a, s):
    pairs = [(i * NZ + k, i * NZ + (k + s) % NZ) for i in range(NY) for k in range(NZ)]
    return lax.ppermute(a, "prefix", pairs)


def core_swap(a):
    return lax.ppermute(a, "resp", [(i, i ^ 1) for i in range(16)])


def x_shift(a, s):
    pairs = [(h * 8 + x * 2 + c, h * 8 + (x + s) % 4 * 2 + c) for h in range(2) for x in range(4) for c in range(2)]
    return lax.ppermute(a, "resp", pairs)


def far_swap(a):
    return lax.ppermute(a, "resp", [(i, i ^ 8) for i in range(16)])


def over_responses(partial):
    core = lax.axis_index("resp") % 2
    mine = lax.dynamic_index_in_dim(partial, core, 0, keepdims=False)
    other = lax.dynamic_index_in_dim(partial, 1 - core, 0, keepdims=False)
    half = (mine + core_swap(other)).astype(BF16)
    near, across, back = (x_shift(half, s).astype(F32) for s in (1, 2, 3))
    half = (half.astype(F32) + across) + (near + back)
    low = half.astype(BF16)
    half = low.astype(F32) + far_swap(low).astype(F32)
    other = core_swap(half)
    return jnp.where(core == 0, half, other), jnp.where(core == 0, other, half)


def per_device(
    response_queries,
    response_keys,
    response_values,
    prompt_keys,
    prompt_values,
    output_grad,
    lengths,
):
    prefix = lax.axis_index("prefix")
    y, z = prefix // NZ, prefix % NZ
    info = jnp.stack([y, z, lengths[lax.axis_index("resp")]]).astype(jnp.int32)

    def split(a, s, width):
        return lax.dynamic_slice_in_dim(a, (y + s) % NY * width, width, a.ndim - 1)

    keyvals = jnp.stack(
        [
            jnp.concatenate([prompt_keys, response_keys[0]], axis=0),
            jnp.concatenate([prompt_values, response_values[0]], axis=0),
        ]
    )
    by_y = [split(keyvals, s, HD) for s in range(NY)]
    by_y = [by_y[0]] + [y_shift(by_y[s], s) for s in range(1, NY)]
    ordered = lax.dynamic_index_in_dim
    stacked = jnp.stack(by_y)
    own = jnp.stack([ordered(stacked, (y - b) % NY, 0, keepdims=False) for b in range(NY)])
    keyvals = [own] + [z_shift(own, s) for s in range(1, NZ)]
    width = HEADS * HD
    queries = [split(response_queries[0], s, width) for s in range(NY)]
    queries = [queries[0]] + [y_shift(queries[s], s) for s in range(1, NY)]
    grads = [split(output_grad[0], s, width) for s in range(NY)]
    grads = [grads[0]] + [y_shift(grads[s], s) for s in range(1, NY)]

    results = attend(info, queries, grads, keyvals)
    att, dq, dkv = results[:4], results[4:8], results[8:]
    att = [att[0]] + [y_shift(att[s], s) for s in range(1, NY)]
    dq = [dq[0]] + [y_shift(dq[s], s) for s in range(1, NY)]
    summed = dkv[0].astype(F32) + sum(z_shift(dkv[s], s).astype(F32) for s in range(1, NZ))
    summed = summed.astype(BF16)
    pieces = [ordered(summed, (y + s) % NY, 0, keepdims=False) for s in range(NY)]
    pieces = [pieces[0]] + [y_shift(pieces[s], s) for s in range(1, NY)]
    key_own, value_own, prompt = place_keys(info, pieces)
    prompt_key_grad, prompt_value_grad = over_responses(prompt)
    attention_out, query_grad = place_rows(info, att, dq)
    return (
        attention_out[None],
        query_grad[None],
        key_own[None],
        value_own[None],
        prompt_key_grad,
        prompt_value_grad,
    )


def solution(mesh):
    return jax.shard_map(
        per_device,
        mesh=mesh,
        in_specs=(
            P("resp", "prefix", None),
            P("resp", "prefix", None),
            P("resp", "prefix", None),
            P("prefix", None),
            P("prefix", None),
            P("resp", "prefix", None),
            P(),
        ),
        out_specs=(
            P("resp", "prefix", None),
            P("resp", "prefix", None),
            P("resp", "prefix", None),
            P("resp", "prefix", None),
            P("prefix", None),
            P("prefix", None),
        ),
        check_vma=False,
    )
```

```python
import math

import jax
import jax.numpy as jnp
from jax import lax
from jax.experimental import pallas as pl
from jax.experimental.pallas import tpu as pltpu
from jax.sharding import PartitionSpec as P

HD = 128
BLOCK = 128
PROMPT_ROWS = 48
PIECE = PROMPT_ROWS + BLOCK
HEADS = 5
NY = 4
NZ = 4
PROMPT = PROMPT_ROWS * NY * NZ
KEYS = PROMPT + BLOCK * NY * NZ
ROWS = NY * HEADS * BLOCK
CHUNK = 256
TILE = 256
MASKED = -1e30
SCALE = 1.0 / math.sqrt(HD)
SCALE2 = SCALE * math.log2(math.e)
F32 = jnp.float32
BF16 = jnp.bfloat16
CLASSES = ((0, 2, 2, 0), (2, 5, 4, 0), (5, 7, 6, 4), (7, 10, 8, 4))
PROMPT_CHUNKS = PROMPT // CHUNK
TILES = ROWS // TILE
RESP = KEYS - PROMPT
VMEM = pl.BlockSpec(memory_space=pltpu.VMEM)
SMEM = pl.BlockSpec(memory_space=pltpu.SMEM)


def shaped(shape, dtype):
    return jax.ShapeDtypeStruct(shape, dtype)


def aligned(start, size):
    return pl.ds(pl.multiple_of(start, size), size)


def tile_positions(tile, z):
    u = tile * 2
    lane = lax.broadcasted_iota(jnp.int32, (1, TILE), 1)
    low = (u // HEADS * NZ + z) * BLOCK
    high = ((u + 1) // HEADS * NZ + z) * BLOCK - BLOCK
    return low, lane + jnp.where(lane < BLOCK, low, high)


def causal(s, chunk, query_pos):
    key_pos = lax.broadcasted_iota(jnp.int32, (CHUNK, TILE), 0) + chunk * CHUNK
    return jnp.where(key_pos <= query_pos, s, MASKED)


def fold(a):
    return a.reshape(CHUNK // 8, 8, TILE)


def chunk_rows(c):
    return slice(c * CHUNK, (c + 1) * CHUNK)


def over_tiles(body):
    for first, last, chunks, first_masked in CLASSES:

        def step(tile, carry, chunks=chunks, first_masked=first_masked):
            body(tile, chunks, first_masked)
            return carry

        lax.fori_loop(first, last, step, 0)


def forward_kernel(
    info,
    x0, x1, x2, x3,
    kv0, kv1, kv2, kv3,
    r0, r1, r2, r3,
    os, qs, gs, ks, vs, kt, tops, deltas, dq_part,
    kp, vp, kpt, vpt, vt, sc, pm, dk, dv,
):
    y = info[0]
    z = info[1]
    length = info[2]
    for s, x in enumerate((x0, x1, x2, x3)):
        block = lax.rem(y - s + NY, NY)
        start = (block * NZ + z) * BLOCK
        valid = (lax.broadcasted_iota(jnp.int32, (BLOCK, HD), 0) + start) < length
        for j in range(HEADS):
            at = aligned((block * HEADS + j) * BLOCK, BLOCK)
            cols = slice(j * HD, (j + 1) * HD)
            qs[at, :] = x[0, :, cols]
            gs[at, :] = jnp.where(valid, x[1, :, cols].astype(F32), 0.0).astype(BF16)
    for s, kv in enumerate((kv0, kv1, kv2, kv3)):
        zp = lax.rem(z - s + NZ, NZ)
        for b in range(NY):
            at = aligned((zp * NY + b) * PROMPT_ROWS, PROMPT_ROWS)
            kp[at, :] = kv[b, 0, :PROMPT_ROWS, :]
            vp[at, :] = kv[b, 1, :PROMPT_ROWS, :]
            at = aligned((b * NZ + zp) * BLOCK, BLOCK)
            k = kv[b, 0, PROMPT_ROWS:, :]
            v = kv[b, 1, PROMPT_ROWS:, :]
            ks[at, :] = k
            vs[at, :] = v
            kt[:, at] = k.T
            vt[:, at] = v.T
    for c in range(PROMPT_CHUNKS):
        rows = chunk_rows(c)
        kpt[:, rows] = kp[rows, :].T
        vpt[:, rows] = vp[rows, :].T
    dk[...] = jnp.zeros_like(dk)
    dv[...] = jnp.zeros_like(dv)

    def tile_step(tile, chunks, first_masked):
        at = aligned(tile * TILE, TILE)
        low_pos, query_pos = tile_positions(tile, z)

        @pl.when(low_pos < length)
        def _():
            q = qs[at, :]
            qt = q.T
            top = jnp.full((8, TILE), MASKED, F32)
            for c in range(-PROMPT_CHUNKS, chunks):
                k = kp[chunk_rows(c + PROMPT_CHUNKS), :] if c < 0 else ks[chunk_rows(c), :]
                s = jnp.dot(k, qt, preferred_element_type=F32)
                if c >= first_masked:
                    s = causal(s, c, query_pos)
                sc[chunk_rows(c + PROMPT_CHUNKS), :] = s
                top = jnp.maximum(top, jnp.max(fold(s), axis=0))
            top = jnp.max(top, axis=0, keepdims=True)
            total = jnp.zeros((8, TILE), F32)
            out_t = jnp.zeros((HD, TILE), F32)
            for c in range(-PROMPT_CHUNKS, chunks):
                p = jnp.exp2((sc[chunk_rows(c + PROMPT_CHUNKS), :] - top) * SCALE2)
                total = total + jnp.sum(fold(p), axis=0)
                low = p.astype(BF16)
                if c < 0:
                    pm[chunk_rows(c + PROMPT_CHUNKS), :] = low
                    v = vpt[:, chunk_rows(c + PROMPT_CHUNKS)]
                else:
                    v = vt[:, chunk_rows(c)]
                out_t = out_t + jnp.dot(v, low, preferred_element_type=F32)
            inv = 1.0 / jnp.sum(total, axis=0, keepdims=True)
            out_t = out_t * inv
            os[at, :] = jnp.where(query_pos < length, out_t, 0.0).T.astype(BF16)
            grad_t = gs[at, :].astype(F32).T
            delta = jnp.sum(grad_t * out_t, axis=0, keepdims=True) * inv
            grad_t = grad_t * inv
            grad = grad_t.T.astype(BF16)
            grad_t = grad_t.astype(BF16)
            gs[at, :] = grad
            stat = aligned(tile * 8, 8)
            tops[stat, :] = jnp.broadcast_to(top, (8, TILE))
            deltas[stat, :] = jnp.broadcast_to(delta, (8, TILE))
            dq_t = jnp.zeros((HD, TILE), F32)
            for c in range(PROMPT_CHUNKS):
                rows = chunk_rows(c)
                dp = jnp.dot(vp[rows, :], grad_t, preferred_element_type=F32)
                low = pm[rows, :]
                ds = (low.astype(F32) * (dp - delta)).astype(BF16)
                dv[rows, :] += jnp.dot(low, grad, preferred_element_type=F32)
                dk[rows, :] += jnp.dot(ds, q, preferred_element_type=F32)
                dq_t = dq_t + jnp.dot(kpt[:, rows], ds, preferred_element_type=F32)
            dq_part[aligned(tile * HD, HD), :] = dq_t

        @pl.when(low_pos >= length)
        def _():
            os[at, :] = jnp.zeros((TILE, HD), BF16)

    over_tiles(tile_step)
    for s, r in enumerate((r0, r1, r2, r3)):
        zp = lax.rem(z + s, NZ)
        for b in range(NY):
            at = aligned((zp * NY + b) * PROMPT_ROWS, PROMPT_ROWS)
            r[b, 0] = (dk[at, :] * SCALE).astype(BF16)
            r[b, 1] = dv[at, :].astype(BF16)


def forward(info, rows, keyvals):
    return pl.pallas_call(
        forward_kernel,
        out_shape=[shaped((NY, 2, PROMPT_ROWS, HD), BF16)] * 4
        + [
            shaped((ROWS, HD), BF16),
            shaped((ROWS, HD), BF16),
            shaped((ROWS, HD), BF16),
            shaped((RESP, HD), BF16),
            shaped((RESP, HD), BF16),
            shaped((HD, RESP), BF16),
            shaped((TILES * 8, TILE), F32),
            shaped((TILES * 8, TILE), F32),
            shaped((TILES * HD, TILE), F32),
        ],
        in_specs=[SMEM] + [VMEM] * 8,
        out_specs=[VMEM] * 13,
        scratch_shapes=[
            pltpu.VMEM((PROMPT, HD), BF16),
            pltpu.VMEM((PROMPT, HD), BF16),
            pltpu.VMEM((HD, PROMPT), BF16),
            pltpu.VMEM((HD, PROMPT), BF16),
            pltpu.VMEM((HD, RESP), BF16),
            pltpu.VMEM((KEYS, TILE), F32),
            pltpu.VMEM((PROMPT, TILE), BF16),
            pltpu.VMEM((PROMPT, HD), F32),
            pltpu.VMEM((PROMPT, HD), F32),
        ],
        cost_estimate=pl.CostEstimate(
            flops=16 * 10**9, bytes_accessed=8 * 2**20, transcendentals=5 * 10**6
        ),
        compiler_params=pltpu.CompilerParams(vmem_limit_bytes=40 * 2**20),
        name="forward",
    )(info, *rows, *keyvals)


def backward_kernel(
    info, os, qs, gs, ks, vs, kt, tops, deltas, dq_part,
    d0, d1, d2, d3,
    r0, r1, r2, r3,
    dk, dv, dq,
):
    y = info[0]
    z = info[1]
    length = info[2]
    dk[...] = jnp.zeros_like(dk)
    dv[...] = jnp.zeros_like(dv)

    def tile_step(tile, chunks, first_masked):
        at = aligned(tile * TILE, TILE)
        low_pos, query_pos = tile_positions(tile, z)

        @pl.when(low_pos < length)
        def _():
            q = qs[at, :]
            qt = q.T
            grad = gs[at, :]
            grad_t = grad.T
            stat = aligned(tile * 8, 8)
            top = tops[stat, :][:1]
            delta = deltas[stat, :][:1]
            dq_t = dq_part[aligned(tile * HD, HD), :]
            for c in range(chunks):
                rows = chunk_rows(c)
                s = jnp.dot(ks[rows, :], qt, preferred_element_type=F32)
                if c >= first_masked:
                    s = causal(s, c, query_pos)
                p = jnp.exp2((s - top) * SCALE2)
                dp = jnp.dot(vs[rows, :], grad_t, preferred_element_type=F32)
                ds = (p * (dp - delta)).astype(BF16)
                dv[rows, :] += jnp.dot(p.astype(BF16), grad, preferred_element_type=F32)
                dk[rows, :] += jnp.dot(ds, q, preferred_element_type=F32)
                dq_t = dq_t + jnp.dot(kt[:, rows], ds, preferred_element_type=F32)
            dq[at, :] = (dq_t * SCALE).T.astype(BF16)

        @pl.when(low_pos >= length)
        def _():
            dq[at, :] = jnp.zeros((TILE, HD), BF16)

    over_tiles(tile_step)
    for s, d in enumerate((d0, d1, d2, d3)):
        block = lax.rem(y + s, NY)
        for j in range(HEADS):
            at = aligned((block * HEADS + j) * BLOCK, BLOCK)
            cols = slice(j * HD, (j + 1) * HD)
            d[0, :, cols] = os[at, :]
            d[1, :, cols] = dq[at, :]
    for s, r in enumerate((r0, r1, r2, r3)):
        zp = lax.rem(z + s, NZ)
        for b in range(NY):
            at = aligned((b * NZ + zp) * BLOCK, BLOCK)
            r[b, 0] = (dk[at, :] * SCALE).astype(BF16)
            r[b, 1] = dv[at, :].astype(BF16)


def backward(info, state):
    return pl.pallas_call(
        backward_kernel,
        out_shape=[shaped((2, BLOCK, HEADS * HD), BF16)] * 4
        + [shaped((NY, 2, BLOCK, HD), BF16)] * 4,
        in_specs=[SMEM] + [VMEM] * 9,
        out_specs=[VMEM] * 8,
        scratch_shapes=[
            pltpu.VMEM((RESP, HD), F32),
            pltpu.VMEM((RESP, HD), F32),
            pltpu.VMEM((ROWS, HD), BF16),
        ],
        cost_estimate=pl.CostEstimate(
            flops=16 * 10**9, bytes_accessed=8 * 2**20, transcendentals=5 * 10**6
        ),
        compiler_params=pltpu.CompilerParams(vmem_limit_bytes=40 * 2**20),
        name="backward",
    )(info, *state)


def settle_kernel(
    info,
    d0, d1, d2, d3,
    r0, r1, r2, r3,
    a, d, p0, p1, p2, p3,
):
    y = info[0]
    width = HEADS * HD
    for s, rows in enumerate((d0, d1, d2, d3)):
        at = aligned(lax.rem(y - s + NY, NY) * width, width)
        a[:, at] = rows[0]
        d[:, at] = rows[1]
    for s, p in enumerate((p0, p1, p2, p3)):
        b = lax.rem(y + s, NY)
        p[...] = (
            (r0[b].astype(F32) + r1[b].astype(F32)) + (r2[b].astype(F32) + r3[b].astype(F32))
        ).astype(BF16)


def settle(info, rows, terms):
    out = shaped((BLOCK, NY * HEADS * HD), BF16)
    return pl.pallas_call(
        settle_kernel,
        out_shape=[out, out] + [shaped((2, BLOCK, HD), BF16)] * 4,
        in_specs=[SMEM] + [VMEM] * 8,
        out_specs=[VMEM] * 6,
        name="settle",
    )(info, *rows, *terms)


def place_kernel(info, p0, p1, p2, p3, dk, dv):
    y = info[0]
    for s, p in enumerate((p0, p1, p2, p3)):
        at = aligned(lax.rem(y - s + NY, NY) * HD, HD)
        dk[:, at] = p[0].astype(F32)
        dv[:, at] = p[1].astype(F32)


def place(info, pieces):
    rows = pieces[0].shape[1]
    out = shaped((rows, NY * HD), F32)
    return pl.pallas_call(
        place_kernel,
        out_shape=[out, out],
        in_specs=[SMEM] + [VMEM] * 4,
        out_specs=[VMEM] * 2,
        name="place",
    )(info, *pieces)


def y_shift(a, s):
    pairs = [(i * NZ + k, (i + s) % NY * NZ + k) for i in range(NY) for k in range(NZ)]
    return lax.ppermute(a, "prefix", pairs)


def z_shift(a, s):
    pairs = [(i * NZ + k, i * NZ + (k + s) % NZ) for i in range(NY) for k in range(NZ)]
    return lax.ppermute(a, "prefix", pairs)


def core_swap(a):
    return lax.ppermute(a, "resp", [(i, i ^ 1) for i in range(16)])


def x_shift(a, s):
    pairs = [(h * 8 + x * 2 + c, h * 8 + (x + s) % 4 * 2 + c) for h in range(2) for x in range(4) for c in range(2)]
    return lax.ppermute(a, "resp", pairs)


def far_swap(a):
    return lax.ppermute(a, "resp", [(i, i ^ 8) for i in range(16)])


def over_responses(dk, dv):
    core = lax.axis_index("resp") % 2
    half = (jnp.where(core == 0, dk, dv) + core_swap(jnp.where(core == 0, dv, dk))).astype(BF16)
    near, across, back = (x_shift(half, s).astype(F32) for s in (1, 2, 3))
    low = ((half.astype(F32) + across) + (near + back)).astype(BF16)
    half = low.astype(F32) + far_swap(low).astype(F32)
    other = core_swap(half)
    return jnp.where(core == 0, half, other), jnp.where(core == 0, other, half)


def by_y(pieces):
    return [pieces[0]] + [y_shift(pieces[s], s) for s in range(1, NY)]


def by_z(pieces):
    return [pieces[0]] + [z_shift(pieces[s], s) for s in range(1, NZ)]


def per_device(
    response_queries,
    response_keys,
    response_values,
    prompt_keys,
    prompt_values,
    output_grad,
    lengths,
):
    prefix = lax.axis_index("prefix")
    y, z = prefix // NZ, prefix % NZ
    info = jnp.stack([y, z, lengths[lax.axis_index("resp")]]).astype(jnp.int32)
    pick = lax.dynamic_index_in_dim

    def split(a, width):
        return [
            lax.dynamic_slice_in_dim(a, (y + s) % NY * width, width, a.ndim - 1)
            for s in range(NY)
        ]

    keyvals = jnp.stack(
        [
            jnp.concatenate([prompt_keys, response_keys[0]], axis=0),
            jnp.concatenate([prompt_values, response_values[0]], axis=0),
        ]
    )
    keyvals = by_y(split(keyvals, HD))
    *keyvals, queries, grads = lax.optimization_barrier(
        (*keyvals, response_queries[0], output_grad[0])
    )
    stacked = jnp.stack(keyvals)
    keyvals = jnp.stack([pick(stacked, (y - b) % NY, 0, keepdims=False) for b in range(NY)])
    keyvals = by_z([keyvals] * NZ)
    rows = by_y(split(jnp.stack([queries, grads]), HEADS * HD))

    *prompt_terms, os, qs, gs, ks, vs, kt, tops, deltas, dq_part = forward(info, rows, keyvals)
    prompt_terms = by_z(prompt_terms)
    back = backward(info, (os, qs, gs, ks, vs, kt, tops, deltas, dq_part))
    *prompt_terms, rows_first, back_first = lax.optimization_barrier(
        (*prompt_terms, back[0], back[4])
    )
    rows = by_y([rows_first, *back[1:4]])
    terms = by_z([back_first, *back[5:]])
    prompt = sum(t.astype(F32) for t in prompt_terms).astype(BF16)
    prompt = by_y([pick(prompt, (y + s) % NY, 0, keepdims=False) for s in range(NY)])
    prompt_key_grad, prompt_value_grad = over_responses(*place(info, prompt))
    attention_out, query_grad, *pieces = settle(info, rows, terms)
    key_own, value_own = place(info, by_y(pieces))
    return (
        attention_out[None],
        query_grad[None],
        key_own[None],
        value_own[None],
        prompt_key_grad,
        prompt_value_grad,
    )


def solution(mesh):
    return jax.shard_map(
        per_device,
        mesh=mesh,
        in_specs=(
            P("resp", "prefix", None),
            P("resp", "prefix", None),
            P("resp", "prefix", None),
            P("prefix", None),
            P("prefix", None),
            P("resp", "prefix", None),
            P(),
        ),
        out_specs=(
            P("resp", "prefix", None),
            P("resp", "prefix", None),
            P("resp", "prefix", None),
            P("resp", "prefix", None),
            P("prefix", None),
            P("prefix", None),
        ),
        check_vma=False,
    )
```

```python
import math

import jax
import jax.numpy as jnp
from jax import lax
from jax.experimental import pallas as pl
from jax.experimental.pallas import tpu as pltpu
from jax.sharding import PartitionSpec as P

HD = 128
BLOCK = 128
PROMPT_ROWS = 48
PIECE = PROMPT_ROWS + BLOCK
HEADS = 5
NY = 4
NZ = 4
PROMPT = PROMPT_ROWS * NY * NZ
KEYS = PROMPT + BLOCK * NY * NZ
ROWS = NY * HEADS * BLOCK
CHUNK = 256
TILE = 256
MASKED = -1e30
SCALE = 1.0 / math.sqrt(HD)
SCALE2 = SCALE * math.log2(math.e)
F32 = jnp.float32
BF16 = jnp.bfloat16
CLASSES = ((0, 2, 2, 0), (2, 5, 4, 0), (5, 7, 6, 4), (7, 10, 8, 4))
PROMPT_CHUNKS = PROMPT // CHUNK
TILES = ROWS // TILE
RESP = KEYS - PROMPT
GROUP = HEADS * BLOCK
VMEM = pl.BlockSpec(memory_space=pltpu.VMEM)
SMEM = pl.BlockSpec(memory_space=pltpu.SMEM)


def shaped(shape, dtype):
    return jax.ShapeDtypeStruct(shape, dtype)


def aligned(start, size):
    return pl.ds(pl.multiple_of(start, size), size)


def head_rows(block):
    return aligned(lax.rem(block, NY) * GROUP, GROUP)


def tile_positions(tile, z):
    u = tile * 2
    lane = lax.broadcasted_iota(jnp.int32, (1, TILE), 1)
    low = (u // HEADS * NZ + z) * BLOCK
    high = ((u + 1) // HEADS * NZ + z) * BLOCK - BLOCK
    return low, lane + jnp.where(lane < BLOCK, low, high)


def causal(s, chunk, query_pos):
    key_pos = lax.broadcasted_iota(jnp.int32, (CHUNK, TILE), 0) + chunk * CHUNK
    return jnp.where(key_pos <= query_pos, s, MASKED)


def fold(a):
    return a.reshape(CHUNK // 8, 8, TILE)


def chunk_rows(c):
    return slice(c * CHUNK, (c + 1) * CHUNK)


def over_tiles(body):
    for first, last, chunks, first_masked in CLASSES:

        def step(tile, carry, chunks=chunks, first_masked=first_masked):
            body(tile, chunks, first_masked)
            return carry

        lax.fori_loop(first, last, step, 0)


def forward_kernel(
    info,
    x0, x1, x2, x3,
    kv0, kv1, kv2, kv3,
    r0, r1, r2, r3,
    a1, a3, os, qs, gs, ks, vs, kt, tops, deltas, dq_part,
    kp, vp, kpt, vpt, vt, sc, pm, dk, dv,
):
    y = info[0]
    z = info[1]
    length = info[2]
    for s, x in enumerate((x0, x1, x2, x3)):
        block = lax.rem(y - s + NY, NY)
        start = (block * NZ + z) * BLOCK
        valid = (lax.broadcasted_iota(jnp.int32, (BLOCK, HD), 0) + start) < length
        for j in range(HEADS):
            at = aligned((block * HEADS + j) * BLOCK, BLOCK)
            cols = slice(j * HD, (j + 1) * HD)
            qs[at, :] = x[0, :, cols]
            gs[at, :] = jnp.where(valid, x[1, :, cols].astype(F32), 0.0).astype(BF16)
    for s, kv in enumerate((kv0, kv1, kv2, kv3)):
        zp = lax.rem(z - s + NZ, NZ)
        for b in range(NY):
            at = aligned((zp * NY + b) * PROMPT_ROWS, PROMPT_ROWS)
            kp[at, :] = kv[b, 0, :PROMPT_ROWS, :]
            vp[at, :] = kv[b, 1, :PROMPT_ROWS, :]
            at = aligned((b * NZ + zp) * BLOCK, BLOCK)
            k = kv[b, 0, PROMPT_ROWS:, :]
            v = kv[b, 1, PROMPT_ROWS:, :]
            ks[at, :] = k
            vs[at, :] = v
            kt[:, at] = k.T
            vt[:, at] = v.T
    for c in range(PROMPT_CHUNKS):
        rows = chunk_rows(c)
        kpt[:, rows] = kp[rows, :].T
        vpt[:, rows] = vp[rows, :].T
    dk[...] = jnp.zeros_like(dk)
    dv[...] = jnp.zeros_like(dv)

    def tile_step(tile, chunks, first_masked):
        at = aligned(tile * TILE, TILE)
        low_pos, query_pos = tile_positions(tile, z)

        @pl.when(low_pos < length)
        def _():
            q = qs[at, :]
            qt = q.T
            top = jnp.full((8, TILE), MASKED, F32)
            for c in range(-PROMPT_CHUNKS, chunks):
                k = kp[chunk_rows(c + PROMPT_CHUNKS), :] if c < 0 else ks[chunk_rows(c), :]
                s = jnp.dot(k, qt, preferred_element_type=F32)
                if c >= first_masked:
                    s = causal(s, c, query_pos)
                sc[chunk_rows(c + PROMPT_CHUNKS), :] = s
                top = jnp.maximum(top, jnp.max(fold(s), axis=0))
            top = jnp.max(top, axis=0, keepdims=True)
            total = jnp.zeros((8, TILE), F32)
            out_t = jnp.zeros((HD, TILE), F32)
            for c in range(-PROMPT_CHUNKS, chunks):
                p = jnp.exp2((sc[chunk_rows(c + PROMPT_CHUNKS), :] - top) * SCALE2)
                total = total + jnp.sum(fold(p), axis=0)
                low = p.astype(BF16)
                if c < 0:
                    pm[chunk_rows(c + PROMPT_CHUNKS), :] = low
                    v = vpt[:, chunk_rows(c + PROMPT_CHUNKS)]
                else:
                    v = vt[:, chunk_rows(c)]
                out_t = out_t + jnp.dot(v, low, preferred_element_type=F32)
            inv = 1.0 / jnp.sum(total, axis=0, keepdims=True)
            out_t = out_t * inv
            os[at, :] = jnp.where(query_pos < length, out_t, 0.0).T.astype(BF16)
            grad_t = gs[at, :].astype(F32).T
            delta = jnp.sum(grad_t * out_t, axis=0, keepdims=True) * inv
            grad_t = grad_t * inv
            grad = grad_t.T.astype(BF16)
            grad_t = grad_t.astype(BF16)
            gs[at, :] = grad
            stat = aligned(tile * 8, 8)
            tops[stat, :] = jnp.broadcast_to(top, (8, TILE))
            deltas[stat, :] = jnp.broadcast_to(delta, (8, TILE))
            dq_t = jnp.zeros((HD, TILE), F32)
            for c in range(PROMPT_CHUNKS):
                rows = chunk_rows(c)
                dp = jnp.dot(vp[rows, :], grad_t, preferred_element_type=F32)
                low = pm[rows, :]
                ds = (low.astype(F32) * (dp - delta)).astype(BF16)
                dv[rows, :] += jnp.dot(low, grad, preferred_element_type=F32)
                dk[rows, :] += jnp.dot(ds, q, preferred_element_type=F32)
                dq_t = dq_t + jnp.dot(kpt[:, rows], ds, preferred_element_type=F32)
            dq_part[aligned(tile * HD, HD), :] = dq_t

        @pl.when(low_pos >= length)
        def _():
            os[at, :] = jnp.zeros((TILE, HD), BF16)

    over_tiles(tile_step)
    a1[...] = os[head_rows(y + 1), :]
    a3[...] = os[head_rows(y + 3), :]
    for s, r in enumerate((r0, r1, r2, r3)):
        zp = lax.rem(z + s, NZ)
        for b in range(NY):
            at = aligned((zp * NY + b) * PROMPT_ROWS, PROMPT_ROWS)
            r[b, 0] = (dk[at, :] * SCALE).astype(BF16)
            r[b, 1] = dv[at, :].astype(BF16)


def forward(info, rows, keyvals):
    return pl.pallas_call(
        forward_kernel,
        out_shape=[shaped((NY, 2, PROMPT_ROWS, HD), BF16)] * 4
        + [shaped((GROUP, HD), BF16)] * 2
        + [
            shaped((ROWS, HD), BF16),
            shaped((ROWS, HD), BF16),
            shaped((ROWS, HD), BF16),
            shaped((RESP, HD), BF16),
            shaped((RESP, HD), BF16),
            shaped((HD, RESP), BF16),
            shaped((TILES * 8, TILE), F32),
            shaped((TILES * 8, TILE), F32),
            shaped((TILES * HD, TILE), F32),
        ],
        in_specs=[SMEM] + [VMEM] * 8,
        out_specs=[VMEM] * 15,
        scratch_shapes=[
            pltpu.VMEM((PROMPT, HD), BF16),
            pltpu.VMEM((PROMPT, HD), BF16),
            pltpu.VMEM((HD, PROMPT), BF16),
            pltpu.VMEM((HD, PROMPT), BF16),
            pltpu.VMEM((HD, RESP), BF16),
            pltpu.VMEM((KEYS, TILE), F32),
            pltpu.VMEM((PROMPT, TILE), BF16),
            pltpu.VMEM((PROMPT, HD), F32),
            pltpu.VMEM((PROMPT, HD), F32),
        ],
        cost_estimate=pl.CostEstimate(
            flops=16 * 10**9, bytes_accessed=8 * 2**20, transcendentals=5 * 10**6
        ),
        compiler_params=pltpu.CompilerParams(vmem_limit_bytes=40 * 2**20),
        name="forward",
    )(info, *rows, *keyvals)


def backward_kernel(
    info, os, qs, gs, ks, vs, kt, tops, deltas, dq_part,
    d0, d1, d2, d3,
    r0, r1, r2, r3,
    dk, dv, dq,
):
    y = info[0]
    z = info[1]
    length = info[2]
    dk[...] = jnp.zeros_like(dk)
    dv[...] = jnp.zeros_like(dv)

    def tile_step(tile, chunks, first_masked):
        at = aligned(tile * TILE, TILE)
        low_pos, query_pos = tile_positions(tile, z)

        @pl.when(low_pos < length)
        def _():
            q = qs[at, :]
            qt = q.T
            grad = gs[at, :]
            grad_t = grad.T
            stat = aligned(tile * 8, 8)
            top = tops[stat, :][:1]
            delta = deltas[stat, :][:1]
            dq_t = dq_part[aligned(tile * HD, HD), :]
            for c in range(chunks):
                rows = chunk_rows(c)
                s = jnp.dot(ks[rows, :], qt, preferred_element_type=F32)
                if c >= first_masked:
                    s = causal(s, c, query_pos)
                p = jnp.exp2((s - top) * SCALE2)
                dp = jnp.dot(vs[rows, :], grad_t, preferred_element_type=F32)
                ds = (p * (dp - delta)).astype(BF16)
                dv[rows, :] += jnp.dot(p.astype(BF16), grad, preferred_element_type=F32)
                dk[rows, :] += jnp.dot(ds, q, preferred_element_type=F32)
                dq_t = dq_t + jnp.dot(kt[:, rows], ds, preferred_element_type=F32)
            dq[at, :] = (dq_t * SCALE).T.astype(BF16)

        @pl.when(low_pos >= length)
        def _():
            dq[at, :] = jnp.zeros((TILE, HD), BF16)

    over_tiles(tile_step)
    for s, d in ((0, d0), (2, d2)):
        d[:GROUP, :] = os[head_rows(y + s), :]
        d[GROUP:, :] = dq[head_rows(y + s), :]
    d1[...] = dq[head_rows(y + 1), :]
    d3[...] = dq[head_rows(y + 3), :]
    for s, r in enumerate((r0, r1, r2, r3)):
        zp = lax.rem(z + s, NZ)
        for b in range(NY):
            at = aligned((b * NZ + zp) * BLOCK, BLOCK)
            r[b, 0] = (dk[at, :] * SCALE).astype(BF16)
            r[b, 1] = dv[at, :].astype(BF16)


def backward(info, state):
    return pl.pallas_call(
        backward_kernel,
        out_shape=[shaped((rows, HD), BF16) for rows in (2 * GROUP, GROUP, 2 * GROUP, GROUP)]
        + [shaped((NY, 2, BLOCK, HD), BF16)] * 4,
        in_specs=[SMEM] + [VMEM] * 9,
        out_specs=[VMEM] * 8,
        scratch_shapes=[
            pltpu.VMEM((RESP, HD), F32),
            pltpu.VMEM((RESP, HD), F32),
            pltpu.VMEM((ROWS, HD), BF16),
        ],
        cost_estimate=pl.CostEstimate(
            flops=16 * 10**9, bytes_accessed=8 * 2**20, transcendentals=5 * 10**6
        ),
        compiler_params=pltpu.CompilerParams(vmem_limit_bytes=40 * 2**20),
        name="backward",
    )(info, *state)


def lay_heads(y, pieces, out):
    for s, (piece, first) in enumerate(pieces):
        block = lax.rem(y - s + NY, NY)
        for j in range(HEADS):
            at = aligned((block * HEADS + j) * HD, HD)
            out[:, at] = piece[first + j * BLOCK : first + (j + 1) * BLOCK, :]


def settle_kernel(
    info, d0, d1, d2, d3, a1, a3, r0, r1, r2, r3, prompt, a, p0, p1, p2, p3
):
    y = info[0]
    lay_heads(y, ((d0, 0), (a1, 0), (d2, 0), (a3, 0)), a)
    for s, p in enumerate((p0, p1, p2, p3)):
        b = lax.rem(y + s, NY)
        for i in range(2):
            p[i * PIECE : i * PIECE + PROMPT_ROWS, :] = prompt[b, i].astype(BF16)
            p[i * PIECE + PROMPT_ROWS : (i + 1) * PIECE, :] = (
                (r0[b, i].astype(F32) + r1[b, i].astype(F32))
                + (r2[b, i].astype(F32) + r3[b, i].astype(F32))
            ).astype(BF16)
    p1[2 * PIECE :, :] = d1[...]
    p3[2 * PIECE :, :] = d3[...]


def settle(info, rows, att, terms, prompt):
    return pl.pallas_call(
        settle_kernel,
        out_shape=[shaped((BLOCK, NY * HEADS * HD), BF16)]
        + [shaped((2 * PIECE + s % 2 * GROUP, HD), BF16) for s in range(NY)],
        in_specs=[SMEM] + [VMEM] * 11,
        out_specs=[VMEM] * 5,
        name="settle",
    )(info, *rows, *att, *terms, prompt)


def place_kernel(info, d0, d2, p0, p1, p2, p3, d, dk, dv, pk, pv):
    y = info[0]
    lay_heads(y, ((d0, GROUP), (p1, 2 * PIECE), (d2, GROUP), (p3, 2 * PIECE)), d)
    for s, p in enumerate((p0, p1, p2, p3)):
        at = aligned(lax.rem(y - s + NY, NY) * HD, HD)
        pk[:, at] = p[:PROMPT_ROWS, :].astype(F32)
        dk[:, at] = p[PROMPT_ROWS:PIECE, :].astype(F32)
        pv[:, at] = p[PIECE : PIECE + PROMPT_ROWS, :].astype(F32)
        dv[:, at] = p[PIECE + PROMPT_ROWS : 2 * PIECE, :].astype(F32)


def place(info, rows, pieces):
    out = shaped((BLOCK, NY * HD), F32)
    prompt_out = shaped((PROMPT_ROWS, NY * HD), F32)
    return pl.pallas_call(
        place_kernel,
        out_shape=[shaped((BLOCK, NY * HEADS * HD), BF16), out, out, prompt_out, prompt_out],
        in_specs=[SMEM] + [VMEM] * 6,
        out_specs=[VMEM] * 5,
        name="place",
    )(info, *rows, *pieces)


def y_shift(a, s):
    pairs = [(i * NZ + k, (i + s) % NY * NZ + k) for i in range(NY) for k in range(NZ)]
    return lax.ppermute(a, "prefix", pairs)


def z_shift(a, s):
    pairs = [(i * NZ + k, i * NZ + (k + s) % NZ) for i in range(NY) for k in range(NZ)]
    return lax.ppermute(a, "prefix", pairs)


def core_swap(a):
    return lax.ppermute(a, "resp", [(i, i ^ 1) for i in range(16)])


def x_swap(a, bit):
    return lax.ppermute(a, "resp", [(i, i ^ (2 * bit)) for i in range(16)])


def far_swap(a):
    return lax.ppermute(a, "resp", [(i, i ^ 8) for i in range(16)])


def over_responses(terms):
    core = lax.axis_index("resp") % 2
    dk, dv = terms[0], terms[1]
    half = jnp.where(core == 0, dk, dv) + core_swap(jnp.where(core == 0, dv, dk))
    for swap in (lambda a: x_swap(a, 1), lambda a: x_swap(a, 2), far_swap):
        low = half.astype(BF16)
        half = low.astype(F32) + swap(low).astype(F32)
    other = core_swap(half.astype(BF16)).astype(F32)
    half = half.astype(BF16).astype(F32)
    return jnp.stack([jnp.where(core == 0, half, other), jnp.where(core == 0, other, half)])


def by_y(pieces):
    return [pieces[0]] + [y_shift(pieces[s], s) for s in range(1, NY)]


def by_z(pieces):
    return [pieces[0]] + [z_shift(pieces[s], s) for s in range(1, NZ)]


def per_device(
    response_queries,
    response_keys,
    response_values,
    prompt_keys,
    prompt_values,
    output_grad,
    lengths,
):
    prefix = lax.axis_index("prefix")
    y, z = prefix // NZ, prefix % NZ
    info = jnp.stack([y, z, lengths[lax.axis_index("resp")]]).astype(jnp.int32)
    pick = lax.dynamic_index_in_dim

    def split(a, width):
        return [
            lax.dynamic_slice_in_dim(a, (y + s) % NY * width, width, a.ndim - 1)
            for s in range(NY)
        ]

    keyvals = jnp.stack(
        [
            jnp.concatenate([prompt_keys, response_keys[0]], axis=0),
            jnp.concatenate([prompt_values, response_values[0]], axis=0),
        ]
    )
    keyvals = by_y(split(keyvals, HD))
    *keyvals, queries, grads = lax.optimization_barrier(
        (*keyvals, response_queries[0], output_grad[0])
    )
    stacked = jnp.stack(keyvals)
    keyvals = jnp.stack([pick(stacked, (y - b) % NY, 0, keepdims=False) for b in range(NY)])
    keyvals = by_z([keyvals] * NZ)
    rows = by_y(split(jnp.stack([queries, grads]), HEADS * HD))

    results = forward(info, rows, keyvals)
    prompt_terms = by_z(results[:4])
    att = [y_shift(results[4], 1), y_shift(results[5], 3)]
    d0, d1, d2, d3, *terms = backward(info, results[6:])
    *prompt_terms, att[0], att[1], d2, terms[1], terms[2], terms[3] = lax.optimization_barrier(
        (*prompt_terms, *att, d2, terms[1], terms[2], terms[3])
    )
    prompt = sum(t.astype(F32) for t in prompt_terms)
    prompt = prompt.transpose(1, 0, 2, 3).reshape(2, NY * PROMPT_ROWS, HD)
    once = jnp.minimum(lengths[0], 1)
    terms = by_z(terms)
    d2 = y_shift(d2, 2)
    prompt = lax.fori_loop(0, once, lambda i, terms: over_responses(terms), prompt)
    prompt = prompt.reshape(2, NY, PROMPT_ROWS, HD).transpose(1, 0, 2, 3)
    attention_out, *pieces = settle(info, (d0, d1, d2, d3), att, terms, prompt)
    query_grad, key_own, value_own, prompt_key_grad, prompt_value_grad = place(
        info, (d0, d2), by_y(pieces)
    )
    return (
        attention_out[None],
        query_grad[None],
        key_own[None],
        value_own[None],
        prompt_key_grad,
        prompt_value_grad,
    )


def solution(mesh):
    return jax.shard_map(
        per_device,
        mesh=mesh,
        in_specs=(
            P("resp", "prefix", None),
            P("resp", "prefix", None),
            P("resp", "prefix", None),
            P("prefix", None),
            P("prefix", None),
            P("resp", "prefix", None),
            P(),
        ),
        out_specs=(
            P("resp", "prefix", None),
            P("resp", "prefix", None),
            P("resp", "prefix", None),
            P("resp", "prefix", None),
            P("prefix", None),
            P("prefix", None),
        ),
        check_vma=False,
    )
```

```python
import math

import jax
import jax.numpy as jnp
from jax import lax
from jax.experimental import pallas as pl
from jax.experimental.pallas import tpu as pltpu
from jax.sharding import PartitionSpec as P

HD = 128
BLOCK = 128
PROMPT_ROWS = 48
PIECE = PROMPT_ROWS + BLOCK
HEADS = 5
NY = 4
NZ = 4
PROMPT = PROMPT_ROWS * NY * NZ
KEYS = PROMPT + BLOCK * NY * NZ
ROWS = NY * HEADS * BLOCK
CHUNK = 256
TILE = 256
MASKED = -1e30
SCALE = 1.0 / math.sqrt(HD)
SCALE2 = SCALE * math.log2(math.e)
F32 = jnp.float32
BF16 = jnp.bfloat16
CLASSES = ((0, 2, 2, 0), (2, 5, 4, 0), (5, 7, 6, 4), (7, 10, 8, 4))
PROMPT_CHUNKS = PROMPT // CHUNK
TILES = ROWS // TILE
RESP = KEYS - PROMPT
GROUP = HEADS * BLOCK
VMEM = pl.BlockSpec(memory_space=pltpu.VMEM)
SMEM = pl.BlockSpec(memory_space=pltpu.SMEM)


def shaped(shape, dtype):
    return jax.ShapeDtypeStruct(shape, dtype)


def aligned(start, size):
    return pl.ds(pl.multiple_of(start, size), size)


def head_rows(block):
    return aligned(lax.rem(block, NY) * GROUP, GROUP)


def tile_positions(tile, z):
    u = tile * 2
    lane = lax.broadcasted_iota(jnp.int32, (1, TILE), 1)
    low = (u // HEADS * NZ + z) * BLOCK
    high = ((u + 1) // HEADS * NZ + z) * BLOCK - BLOCK
    return low, lane + jnp.where(lane < BLOCK, low, high)


def causal(s, chunk, query_pos):
    key_pos = lax.broadcasted_iota(jnp.int32, (CHUNK, TILE), 0) + chunk * CHUNK
    return jnp.where(key_pos <= query_pos, s, MASKED)


def fold(a):
    return a.reshape(CHUNK // 8, 8, TILE)


def chunk_rows(c):
    return slice(c * CHUNK, (c + 1) * CHUNK)


def over_tiles(body):
    for first, last, chunks, first_masked in CLASSES:

        def step(tile, carry, chunks=chunks, first_masked=first_masked):
            body(tile, chunks, first_masked)
            return carry

        lax.fori_loop(first, last, step, 0)


def prompt_kernel(
    info,
    x0, x1, x2, x3,
    mine, other,
    qs, gs, kpt, vp, pm, tops, totals, outs,
    kp, vpt, sc,
):
    y = info[0]
    z = info[1]
    length = info[2]
    core = info[3]
    for s, x in enumerate((x0, x1, x2, x3)):
        block = lax.rem(y - s + NY, NY)
        start = (block * NZ + z) * BLOCK
        valid = (lax.broadcasted_iota(jnp.int32, (BLOCK, HD), 0) + start) < length
        for j in range(HEADS):
            at = aligned((block * HEADS + j) * BLOCK, BLOCK)
            cols = slice(j * HD, (j + 1) * HD)
            qs[at, :] = x[0, :, cols]
            gs[at, :] = jnp.where(valid, x[1, :, cols].astype(F32), 0.0).astype(BF16)

    @pl.when(core == 0)
    def _():
        kp[...] = mine[...]
        vp[...] = other[...]

    @pl.when(core != 0)
    def _():
        kp[...] = other[...]
        vp[...] = mine[...]

    for c in range(PROMPT_CHUNKS):
        rows = chunk_rows(c)
        kpt[:, rows] = kp[rows, :].T
        vpt[:, rows] = vp[rows, :].T

    def step(tile, carry):
        low_pos, _ = tile_positions(tile, z)

        @pl.when(low_pos < length)
        def _():
            qt = qs[aligned(tile * TILE, TILE), :].T
            top = jnp.full((8, TILE), MASKED, F32)
            for c in range(PROMPT_CHUNKS):
                s = jnp.dot(kp[chunk_rows(c), :], qt, preferred_element_type=F32)
                sc[chunk_rows(c), :] = s
                top = jnp.maximum(top, jnp.max(fold(s), axis=0))
            top = jnp.max(top, axis=0, keepdims=True)
            total = jnp.zeros((8, TILE), F32)
            out_t = jnp.zeros((HD, TILE), F32)
            for c in range(PROMPT_CHUNKS):
                p = jnp.exp2((sc[chunk_rows(c), :] - top) * SCALE2)
                total = total + jnp.sum(fold(p), axis=0)
                low = p.astype(BF16)
                pm[aligned(tile * PROMPT + c * CHUNK, CHUNK), :] = low
                out_t = out_t + jnp.dot(vpt[:, chunk_rows(c)], low, preferred_element_type=F32)
            stat = aligned(tile * 8, 8)
            tops[stat, :] = jnp.broadcast_to(top, (8, TILE))
            totals[stat, :] = total
            outs[aligned(tile * HD, HD), :] = out_t

        return carry

    lax.fori_loop(0, TILES, step, 0)


def prompt_forward(info, rows, mine, other):
    return pl.pallas_call(
        prompt_kernel,
        out_shape=[
            shaped((ROWS, HD), BF16),
            shaped((ROWS, HD), BF16),
            shaped((HD, PROMPT), BF16),
            shaped((PROMPT, HD), BF16),
            shaped((TILES * PROMPT, TILE), BF16),
            shaped((TILES * 8, TILE), F32),
            shaped((TILES * 8, TILE), F32),
            shaped((TILES * HD, TILE), F32),
        ],
        in_specs=[SMEM] + [VMEM] * 6,
        out_specs=[VMEM] * 8,
        scratch_shapes=[
            pltpu.VMEM((PROMPT, HD), BF16),
            pltpu.VMEM((HD, PROMPT), BF16),
            pltpu.VMEM((PROMPT, TILE), F32),
        ],
        cost_estimate=pl.CostEstimate(
            flops=10**6, bytes_accessed=2**10, transcendentals=0
        ),
        compiler_params=pltpu.CompilerParams(vmem_limit_bytes=32 * 2**20),
        name="prompt_forward",
    )(info, *rows, mine, other)


def forward_kernel(
    info,
    qs, gs_in, kpt, vp, pm, tops_in, totals, outs,
    kv0, kv1, kv2, kv3,
    r0, r1, r2, r3,
    a1, a3, os, gs, ks, vs, kt, tops, deltas, dq_part,
    vt, sc, dk, dv,
):
    y = info[0]
    z = info[1]
    length = info[2]
    for s, kv in enumerate((kv0, kv1, kv2, kv3)):
        zp = lax.rem(z - s + NZ, NZ)
        for b in range(NY):
            at = aligned((b * NZ + zp) * BLOCK, BLOCK)
            k = kv[b, 0]
            v = kv[b, 1]
            ks[at, :] = k
            vs[at, :] = v
            kt[:, at] = k.T
            vt[:, at] = v.T
    dk[...] = jnp.zeros_like(dk)
    dv[...] = jnp.zeros_like(dv)

    def tile_step(tile, chunks, first_masked):
        at = aligned(tile * TILE, TILE)
        low_pos, query_pos = tile_positions(tile, z)

        @pl.when(low_pos < length)
        def _():
            q = qs[at, :]
            qt = q.T
            stat = aligned(tile * 8, 8)
            first_top = tops_in[stat, :]
            top = first_top
            for c in range(chunks):
                s = jnp.dot(ks[chunk_rows(c), :], qt, preferred_element_type=F32)
                if c >= first_masked:
                    s = causal(s, c, query_pos)
                sc[chunk_rows(c), :] = s
                top = jnp.maximum(top, jnp.max(fold(s), axis=0))
            top = jnp.max(top, axis=0, keepdims=True)
            alpha = jnp.exp2((first_top[:1] - top) * SCALE2)
            total = totals[stat, :] * alpha
            out_t = outs[aligned(tile * HD, HD), :] * alpha
            for c in range(chunks):
                p = jnp.exp2((sc[chunk_rows(c), :] - top) * SCALE2)
                total = total + jnp.sum(fold(p), axis=0)
                low = p.astype(BF16)
                out_t = out_t + jnp.dot(vt[:, chunk_rows(c)], low, preferred_element_type=F32)
            inv = 1.0 / jnp.sum(total, axis=0, keepdims=True)
            out_t = out_t * inv
            os[at, :] = jnp.where(query_pos < length, out_t, 0.0).T.astype(BF16)
            grad_t = gs_in[at, :].astype(F32).T
            delta = jnp.sum(grad_t * out_t, axis=0, keepdims=True) * inv
            grad_t = grad_t * inv
            gs[at, :] = grad_t.T.astype(BF16)
            tops[stat, :] = jnp.broadcast_to(top, (8, TILE))
            deltas[stat, :] = jnp.broadcast_to(delta, (8, TILE))
            grad_t = grad_t * alpha
            grad = grad_t.T.astype(BF16)
            grad_t = grad_t.astype(BF16)
            delta = delta * alpha
            dq_t = jnp.zeros((HD, TILE), F32)
            for c in range(PROMPT_CHUNKS):
                rows = chunk_rows(c)
                dp = jnp.dot(vp[rows, :], grad_t, preferred_element_type=F32)
                low = pm[aligned(tile * PROMPT + c * CHUNK, CHUNK), :]
                ds = (low.astype(F32) * (dp - delta)).astype(BF16)
                dv[rows, :] += jnp.dot(low, grad, preferred_element_type=F32)
                dk[rows, :] += jnp.dot(ds, q, preferred_element_type=F32)
                dq_t = dq_t + jnp.dot(kpt[:, rows], ds, preferred_element_type=F32)
            dq_part[aligned(tile * HD, HD), :] = dq_t

        @pl.when(low_pos >= length)
        def _():
            os[at, :] = jnp.zeros((TILE, HD), BF16)

    over_tiles(tile_step)
    a1[...] = os[head_rows(y + 1), :]
    a3[...] = os[head_rows(y + 3), :]
    for s, r in enumerate((r0, r1, r2, r3)):
        slot = z ^ lax.rem(z + s, NZ)
        for b in range(NY):
            at = aligned((slot * NY + b) * PROMPT_ROWS, PROMPT_ROWS)
            r[b, 0] = (dk[at, :] * SCALE).astype(BF16)
            r[b, 1] = dv[at, :].astype(BF16)


def forward(info, state, keyvals):
    return pl.pallas_call(
        forward_kernel,
        out_shape=[shaped((NY, 2, PROMPT_ROWS, HD), BF16)] * 4
        + [shaped((GROUP, HD), BF16)] * 2
        + [
            shaped((ROWS, HD), BF16),
            shaped((ROWS, HD), BF16),
            shaped((RESP, HD), BF16),
            shaped((RESP, HD), BF16),
            shaped((HD, RESP), BF16),
            shaped((TILES * 8, TILE), F32),
            shaped((TILES * 8, TILE), F32),
            shaped((TILES * HD, TILE), F32),
        ],
        in_specs=[SMEM] + [VMEM] * 12,
        out_specs=[VMEM] * 14,
        scratch_shapes=[
            pltpu.VMEM((HD, RESP), BF16),
            pltpu.VMEM((RESP, TILE), F32),
            pltpu.VMEM((PROMPT, HD), F32),
            pltpu.VMEM((PROMPT, HD), F32),
        ],
        cost_estimate=pl.CostEstimate(
            flops=16 * 10**9, bytes_accessed=8 * 2**20, transcendentals=5 * 10**6
        ),
        compiler_params=pltpu.CompilerParams(vmem_limit_bytes=32 * 2**20),
        name="forward",
    )(info, *state, *keyvals)


def backward_kernel(
    info, os, qs, gs, ks, vs, kt, tops, deltas, dq_part,
    d0, d1, d2, d3,
    r0, r1, r2, r3,
    dk, dv, dq,
):
    y = info[0]
    z = info[1]
    length = info[2]
    dk[...] = jnp.zeros_like(dk)
    dv[...] = jnp.zeros_like(dv)

    def tile_step(tile, chunks, first_masked):
        at = aligned(tile * TILE, TILE)
        low_pos, query_pos = tile_positions(tile, z)

        @pl.when(low_pos < length)
        def _():
            q = qs[at, :]
            qt = q.T
            grad = gs[at, :]
            grad_t = grad.T
            stat = aligned(tile * 8, 8)
            top = tops[stat, :][:1]
            delta = deltas[stat, :][:1]
            dq_t = dq_part[aligned(tile * HD, HD), :]
            for c in range(chunks):
                rows = chunk_rows(c)
                s = jnp.dot(ks[rows, :], qt, preferred_element_type=F32)
                if c >= first_masked:
                    s = causal(s, c, query_pos)
                p = jnp.exp2((s - top) * SCALE2)
                dp = jnp.dot(vs[rows, :], grad_t, preferred_element_type=F32)
                ds = (p * (dp - delta)).astype(BF16)
                dv[rows, :] += jnp.dot(p.astype(BF16), grad, preferred_element_type=F32)
                dk[rows, :] += jnp.dot(ds, q, preferred_element_type=F32)
                dq_t = dq_t + jnp.dot(kt[:, rows], ds, preferred_element_type=F32)
            dq[at, :] = (dq_t * SCALE).T.astype(BF16)

        @pl.when(low_pos >= length)
        def _():
            dq[at, :] = jnp.zeros((TILE, HD), BF16)

    over_tiles(tile_step)
    for s, d in ((0, d0), (2, d2)):
        d[:GROUP, :] = os[head_rows(y + s), :]
        d[GROUP:, :] = dq[head_rows(y + s), :]
    d1[...] = dq[head_rows(y + 1), :]
    d3[...] = dq[head_rows(y + 3), :]
    for s, r in enumerate((r0, r1, r2, r3)):
        zp = lax.rem(z + s, NZ)
        for b in range(NY):
            at = aligned((b * NZ + zp) * BLOCK, BLOCK)
            r[b, 0] = (dk[at, :] * SCALE).astype(BF16)
            r[b, 1] = dv[at, :].astype(BF16)


def backward(info, state):
    return pl.pallas_call(
        backward_kernel,
        out_shape=[shaped((rows, HD), BF16) for rows in (2 * GROUP, GROUP, 2 * GROUP, GROUP)]
        + [shaped((NY, 2, BLOCK, HD), BF16)] * 4,
        in_specs=[SMEM] + [VMEM] * 9,
        out_specs=[VMEM] * 8,
        scratch_shapes=[
            pltpu.VMEM((RESP, HD), F32),
            pltpu.VMEM((RESP, HD), F32),
            pltpu.VMEM((ROWS, HD), BF16),
        ],
        cost_estimate=pl.CostEstimate(
            flops=16 * 10**9, bytes_accessed=8 * 2**20, transcendentals=5 * 10**6
        ),
        compiler_params=pltpu.CompilerParams(vmem_limit_bytes=40 * 2**20),
        name="backward",
    )(info, *state)


def lay_heads(y, pieces, out):
    for s, (piece, first) in enumerate(pieces):
        block = lax.rem(y - s + NY, NY)
        for j in range(HEADS):
            at = aligned((block * HEADS + j) * HD, HD)
            out[:, at] = piece[first + j * BLOCK : first + (j + 1) * BLOCK, :]


def settle_kernel(
    info, d0, d1, d2, d3, a1, a3, r0, r1, r2, r3, prompt, a, p0, p1, p2, p3
):
    y = info[0]
    lay_heads(y, ((d0, 0), (a1, 0), (d2, 0), (a3, 0)), a)
    for s, p in enumerate((p0, p1, p2, p3)):
        b = lax.rem(y + s, NY)
        for i in range(2):
            p[i * PIECE : i * PIECE + PROMPT_ROWS, :] = prompt[b, i].astype(BF16)
            p[i * PIECE + PROMPT_ROWS : (i + 1) * PIECE, :] = (
                (r0[b, i].astype(F32) + r1[b, i].astype(F32))
                + (r2[b, i].astype(F32) + r3[b, i].astype(F32))
            ).astype(BF16)
    p1[2 * PIECE :, :] = d1[...]
    p3[2 * PIECE :, :] = d3[...]


def settle(info, rows, att, terms, prompt):
    return pl.pallas_call(
        settle_kernel,
        out_shape=[shaped((BLOCK, NY * HEADS * HD), BF16)]
        + [shaped((2 * PIECE + s % 2 * GROUP, HD), BF16) for s in range(NY)],
        in_specs=[SMEM] + [VMEM] * 11,
        out_specs=[VMEM] * 5,
        name="settle",
    )(info, *rows, *att, *terms, prompt)


def place_kernel(info, d0, d2, p0, p1, p2, p3, d, dk, dv, pk, pv):
    y = info[0]
    lay_heads(y, ((d0, GROUP), (p1, 2 * PIECE), (d2, GROUP), (p3, 2 * PIECE)), d)
    for s, p in enumerate((p0, p1, p2, p3)):
        at = aligned(lax.rem(y - s + NY, NY) * HD, HD)
        pk[:, at] = p[:PROMPT_ROWS, :].astype(F32)
        dk[:, at] = p[PROMPT_ROWS:PIECE, :].astype(F32)
        pv[:, at] = p[PIECE : PIECE + PROMPT_ROWS, :].astype(F32)
        dv[:, at] = p[PIECE + PROMPT_ROWS : 2 * PIECE, :].astype(F32)


def place(info, rows, pieces):
    out = shaped((BLOCK, NY * HD), F32)
    prompt_out = shaped((PROMPT_ROWS, NY * HD), F32)
    return pl.pallas_call(
        place_kernel,
        out_shape=[shaped((BLOCK, NY * HEADS * HD), BF16), out, out, prompt_out, prompt_out],
        in_specs=[SMEM] + [VMEM] * 6,
        out_specs=[VMEM] * 5,
        name="place",
    )(info, *rows, *pieces)


def y_shift(a, s):
    pairs = [(i * NZ + k, (i + s) % NY * NZ + k) for i in range(NY) for k in range(NZ)]
    return lax.ppermute(a, "prefix", pairs)


def z_shift(a, s):
    pairs = [(i * NZ + k, i * NZ + (k + s) % NZ) for i in range(NY) for k in range(NZ)]
    return lax.ppermute(a, "prefix", pairs)


def z_swap(a, bit):
    return lax.ppermute(a, "prefix", [(i, i ^ bit) for i in range(NY * NZ)])


def core_swap(a):
    return lax.ppermute(a, "resp", [(i, i ^ 1) for i in range(16)])


def x_swap(a, bit):
    return lax.ppermute(a, "resp", [(i, i ^ (2 * bit)) for i in range(16)])


def far_swap(a):
    return lax.ppermute(a, "resp", [(i, i ^ 8) for i in range(16)])


def over_responses(terms):
    core = lax.axis_index("resp") % 2
    dk, dv = terms[0], terms[1]
    half = jnp.where(core == 0, dk, dv) + core_swap(jnp.where(core == 0, dv, dk))
    for swap in (lambda a: x_swap(a, 1), lambda a: x_swap(a, 2), far_swap):
        low = half.astype(BF16)
        half = low.astype(F32) + swap(low).astype(F32)
    other = core_swap(half.astype(BF16)).astype(F32)
    half = half.astype(BF16).astype(F32)
    return jnp.stack([jnp.where(core == 0, half, other), jnp.where(core == 0, other, half)])


def bring_first(state):
    mine, other, x1, x2, x3 = state
    part = NY * PROMPT_ROWS
    pair = jnp.concatenate([mine[:part], z_swap(mine[:part], 1)])
    mine = jnp.concatenate([pair, z_swap(pair, 2)])
    other = core_swap(mine)
    x1, other = lax.optimization_barrier((x1, other))
    x1 = y_shift(x1, 1)
    x2 = y_shift(x2, 2)
    x3, x2 = lax.optimization_barrier((x3, x2))
    return mine, other, x1, x2, y_shift(x3, 3)


def by_y(pieces):
    return [pieces[0]] + [y_shift(pieces[s], s) for s in range(1, NY)]


def by_z(pieces):
    return [pieces[0]] + [z_shift(pieces[s], s) for s in range(1, NZ)]


def per_device(
    response_queries,
    response_keys,
    response_values,
    prompt_keys,
    prompt_values,
    output_grad,
    lengths,
):
    prefix = lax.axis_index("prefix")
    y, z = prefix // NZ, prefix % NZ
    resp = lax.axis_index("resp")
    core = resp % 2
    info = jnp.stack([y, z, lengths[resp], core]).astype(jnp.int32)
    pick = lax.dynamic_index_in_dim

    def split(a, width):
        return [
            lax.dynamic_slice_in_dim(a, (y + s) % NY * width, width, a.ndim - 1)
            for s in range(NY)
        ]

    keyvals = jnp.stack(
        [
            jnp.concatenate([prompt_keys, response_keys[0]], axis=0),
            jnp.concatenate([prompt_values, response_values[0]], axis=0),
        ]
    )
    keyvals = by_y(split(keyvals, HD))
    stacked = jnp.stack(keyvals)
    stacked = jnp.stack([pick(stacked, (y - b) % NY, 0, keepdims=False) for b in range(NY)])
    half = pick(stacked[:, :, :PROMPT_ROWS], core, 1, keepdims=False)
    half = half.reshape(NY * PROMPT_ROWS, HD)
    mine = jnp.concatenate([half] * NZ)
    keyvals = by_z([stacked[:, :, PROMPT_ROWS:]] * NZ)
    x0, *rows = split(jnp.stack([response_queries[0], output_grad[0]]), HEADS * HD)
    once = jnp.minimum(lengths[0], 1)
    mine, other, *rows = lax.fori_loop(
        0, once, lambda i, state: bring_first(state), (mine, mine, *rows)
    )

    qs, *state = prompt_forward(info, (x0, *rows), mine, other)
    results = forward(info, (qs, *state), keyvals)
    prompt_terms = by_z(results[:4])
    att = [y_shift(results[4], 1), y_shift(results[5], 3)]
    d0, d1, d2, d3, *terms = backward(info, (results[6], qs, *results[7:]))
    *prompt_terms, att[0], att[1], d2, terms[1], terms[2], terms[3] = lax.optimization_barrier(
        (*prompt_terms, *att, d2, terms[1], terms[2], terms[3])
    )
    prompt = sum(t.astype(F32) for t in prompt_terms)
    prompt = prompt.transpose(1, 0, 2, 3).reshape(2, NY * PROMPT_ROWS, HD)
    terms = by_z(terms)
    d2 = y_shift(d2, 2)
    prompt = lax.fori_loop(0, once, lambda i, terms: over_responses(terms), prompt)
    prompt = prompt.reshape(2, NY, PROMPT_ROWS, HD).transpose(1, 0, 2, 3)
    attention_out, *pieces = settle(info, (d0, d1, d2, d3), att, terms, prompt)
    query_grad, key_own, value_own, prompt_key_grad, prompt_value_grad = place(
        info, (d0, d2), by_y(pieces)
    )
    return (
        attention_out[None],
        query_grad[None],
        key_own[None],
        value_own[None],
        prompt_key_grad,
        prompt_value_grad,
    )


def solution(mesh):
    return jax.shard_map(
        per_device,
        mesh=mesh,
        in_specs=(
            P("resp", "prefix", None),
            P("resp", "prefix", None),
            P("resp", "prefix", None),
            P("prefix", None),
            P("prefix", None),
            P("resp", "prefix", None),
            P(),
        ),
        out_specs=(
            P("resp", "prefix", None),
            P("resp", "prefix", None),
            P("resp", "prefix", None),
            P("resp", "prefix", None),
            P("prefix", None),
            P("prefix", None),
        ),
        check_vma=False,
    )
```

```python
import math

import jax
import jax.numpy as jnp
from jax import lax
from jax.experimental import pallas as pl
from jax.experimental.pallas import tpu as pltpu
from jax.sharding import PartitionSpec as P

HD = 128
BLOCK = 128
PROMPT_ROWS = 48
PIECE = PROMPT_ROWS + BLOCK
HEADS = 5
NY = 4
NZ = 4
PROMPT = PROMPT_ROWS * NY * NZ
KEYS = PROMPT + BLOCK * NY * NZ
ROWS = NY * HEADS * BLOCK
CHUNK = 256
TILE = 256
MASKED = -1e30
SCALE = 1.0 / math.sqrt(HD)
SCALE2 = SCALE * math.log2(math.e)
F32 = jnp.float32
BF16 = jnp.bfloat16
CLASSES = ((0, 2, 2, 0), (2, 5, 4, 0), (5, 7, 6, 4), (7, 10, 8, 4))
PROMPT_CHUNKS = PROMPT // CHUNK
TILES = ROWS // TILE
RESP = KEYS - PROMPT
GROUP = HEADS * BLOCK
VMEM = pl.BlockSpec(memory_space=pltpu.VMEM)
SMEM = pl.BlockSpec(memory_space=pltpu.SMEM)


def shaped(shape, dtype):
    return jax.ShapeDtypeStruct(shape, dtype)


def aligned(start, size):
    return pl.ds(pl.multiple_of(start, size), size)


def head_rows(block):
    return aligned(lax.rem(block, NY) * GROUP, GROUP)


def tile_positions(tile, z):
    u = tile * 2
    lane = lax.broadcasted_iota(jnp.int32, (1, TILE), 1)
    low = (u // HEADS * NZ + z) * BLOCK
    high = ((u + 1) // HEADS * NZ + z) * BLOCK - BLOCK
    return low, lane + jnp.where(lane < BLOCK, low, high)


def causal(s, chunk, query_pos):
    key_pos = lax.broadcasted_iota(jnp.int32, (CHUNK, TILE), 0) + chunk * CHUNK
    return jnp.where(key_pos <= query_pos, s, MASKED)


def fold(a):
    return a.reshape(CHUNK // 8, 8, TILE)


def chunk_rows(c):
    return slice(c * CHUNK, (c + 1) * CHUNK)


def over_tiles(body):
    for first, last, chunks, first_masked in CLASSES:

        def step(tile, carry, chunks=chunks, first_masked=first_masked):
            body(tile, chunks, first_masked)
            return carry

        lax.fori_loop(first, last, step, 0)


def forward_kernel(
    info,
    x0, x1, x2, x3,
    kv0, kv1, kv2, kv3,
    r0, r1, r2, r3,
    a1, a3, os, qs, gs, ks, vs, kt, tops, deltas, dq_part,
    kp, vp, kpt, vpt, vt, sc, pm, dk, dv,
):
    y = info[0]
    z = info[1]
    length = info[2]
    for s, x in enumerate((x0, x1, x2, x3)):
        block = lax.rem(y - s + NY, NY)
        start = (block * NZ + z) * BLOCK
        valid = (lax.broadcasted_iota(jnp.int32, (BLOCK, HD), 0) + start) < length
        qs[head_rows(block), :] = x[:GROUP, :]
        for j in range(HEADS):
            at = aligned((block * HEADS + j) * BLOCK, BLOCK)
            g = x[GROUP + j * BLOCK : GROUP + (j + 1) * BLOCK, :]
            gs[at, :] = jnp.where(valid, g.astype(F32), 0.0).astype(BF16)
        for slot in range(NZ):
            at = aligned((slot * NY + block) * PROMPT_ROWS, PROMPT_ROWS)
            first = 2 * GROUP + slot * 2 * PROMPT_ROWS
            kp[at, :] = x[first : first + PROMPT_ROWS, :]
            vp[at, :] = x[first + PROMPT_ROWS : first + 2 * PROMPT_ROWS, :]
    for s, kv in enumerate((kv0, kv1, kv2, kv3)):
        zp = lax.rem(z - s + NZ, NZ)
        for b in range(NY):
            at = aligned((b * NZ + zp) * BLOCK, BLOCK)
            k = kv[b, 0]
            v = kv[b, 1]
            ks[at, :] = k
            vs[at, :] = v
            kt[:, at] = k.T
            vt[:, at] = v.T
    for c in range(PROMPT_CHUNKS):
        rows = chunk_rows(c)
        kpt[:, rows] = kp[rows, :].T
        vpt[:, rows] = vp[rows, :].T
    dk[...] = jnp.zeros_like(dk)
    dv[...] = jnp.zeros_like(dv)

    def tile_step(tile, chunks, first_masked):
        at = aligned(tile * TILE, TILE)
        low_pos, query_pos = tile_positions(tile, z)

        @pl.when(low_pos < length)
        def _():
            q = qs[at, :]
            qt = q.T
            top = jnp.full((8, TILE), MASKED, F32)
            for c in range(-PROMPT_CHUNKS, chunks):
                k = kp[chunk_rows(c + PROMPT_CHUNKS), :] if c < 0 else ks[chunk_rows(c), :]
                s = jnp.dot(k, qt, preferred_element_type=F32)
                if c >= first_masked:
                    s = causal(s, c, query_pos)
                sc[chunk_rows(c + PROMPT_CHUNKS), :] = s
                top = jnp.maximum(top, jnp.max(fold(s), axis=0))
            top = jnp.max(top, axis=0, keepdims=True)
            total = jnp.zeros((8, TILE), F32)
            out_t = jnp.zeros((HD, TILE), F32)
            for c in range(-PROMPT_CHUNKS, chunks):
                p = jnp.exp2((sc[chunk_rows(c + PROMPT_CHUNKS), :] - top) * SCALE2)
                total = total + jnp.sum(fold(p), axis=0)
                low = p.astype(BF16)
                if c < 0:
                    pm[chunk_rows(c + PROMPT_CHUNKS), :] = low
                    v = vpt[:, chunk_rows(c + PROMPT_CHUNKS)]
                else:
                    v = vt[:, chunk_rows(c)]
                out_t = out_t + jnp.dot(v, low, preferred_element_type=F32)
            inv = 1.0 / jnp.sum(total, axis=0, keepdims=True)
            out_t = out_t * inv
            os[at, :] = jnp.where(query_pos < length, out_t, 0.0).T.astype(BF16)
            grad_t = gs[at, :].astype(F32).T
            delta = jnp.sum(grad_t * out_t, axis=0, keepdims=True) * inv
            grad_t = grad_t * inv
            grad = grad_t.T.astype(BF16)
            grad_t = grad_t.astype(BF16)
            gs[at, :] = grad
            stat = aligned(tile * 8, 8)
            tops[stat, :] = jnp.broadcast_to(top, (8, TILE))
            deltas[stat, :] = jnp.broadcast_to(delta, (8, TILE))
            dq_t = jnp.zeros((HD, TILE), F32)
            for c in range(PROMPT_CHUNKS):
                rows = chunk_rows(c)
                dp = jnp.dot(vp[rows, :], grad_t, preferred_element_type=F32)
                low = pm[rows, :]
                ds = (low.astype(F32) * (dp - delta)).astype(BF16)
                dv[rows, :] += jnp.dot(low, grad, preferred_element_type=F32)
                dk[rows, :] += jnp.dot(ds, q, preferred_element_type=F32)
                dq_t = dq_t + jnp.dot(kpt[:, rows], ds, preferred_element_type=F32)
            dq_part[aligned(tile * HD, HD), :] = dq_t

        @pl.when(low_pos >= length)
        def _():
            os[at, :] = jnp.zeros((TILE, HD), BF16)

    over_tiles(tile_step)
    a1[...] = os[head_rows(y + 1), :]
    a3[...] = os[head_rows(y + 3), :]
    for s, r in enumerate((r0, r1, r2, r3)):
        slot = -s % NZ
        for b in range(NY):
            at = slice((slot * NY + b) * PROMPT_ROWS, (slot * NY + b + 1) * PROMPT_ROWS)
            r[b, 0] = (dk[at, :] * SCALE).astype(BF16)
            r[b, 1] = dv[at, :].astype(BF16)


def pack_kernel(info, q, g, k0, k1, k2, k3, x0, x1, x2, x3):
    y = info[0]
    for s, x in enumerate((x0, x1, x2, x3)):
        dest = lax.rem(y + s, NY)
        for j in range(HEADS):
            at = aligned((dest * HEADS + j) * HD, HD)
            x[j * BLOCK : (j + 1) * BLOCK, :] = q[:, at]
            x[GROUP + j * BLOCK : GROUP + (j + 1) * BLOCK, :] = g[:, at]
        for slot, k in enumerate((k0, k1, k2, k3)):
            first = 2 * GROUP + slot * 2 * PROMPT_ROWS
            for i in range(2):
                rows = slice(first + i * PROMPT_ROWS, first + (i + 1) * PROMPT_ROWS)
                x[rows, :] = k[i, :, aligned(dest * HD, HD)]


def pack(info, queries, grads, prompt):
    out = shaped((2 * GROUP + 2 * NZ * PROMPT_ROWS, HD), BF16)
    return pl.pallas_call(
        pack_kernel,
        out_shape=[out] * NY,
        in_specs=[SMEM] + [VMEM] * 6,
        out_specs=[VMEM] * NY,
        name="pack",
    )(info, queries, grads, *prompt)


def forward(info, rows, keyvals):
    return pl.pallas_call(
        forward_kernel,
        out_shape=[shaped((NY, 2, PROMPT_ROWS, HD), BF16)] * 4
        + [shaped((GROUP, HD), BF16)] * 2
        + [
            shaped((ROWS, HD), BF16),
            shaped((ROWS, HD), BF16),
            shaped((ROWS, HD), BF16),
            shaped((RESP, HD), BF16),
            shaped((RESP, HD), BF16),
            shaped((HD, RESP), BF16),
            shaped((TILES * 8, TILE), F32),
            shaped((TILES * 8, TILE), F32),
            shaped((TILES * HD, TILE), F32),
        ],
        in_specs=[SMEM] + [VMEM] * 8,
        out_specs=[VMEM] * 15,
        scratch_shapes=[
            pltpu.VMEM((PROMPT, HD), BF16),
            pltpu.VMEM((PROMPT, HD), BF16),
            pltpu.VMEM((HD, PROMPT), BF16),
            pltpu.VMEM((HD, PROMPT), BF16),
            pltpu.VMEM((HD, RESP), BF16),
            pltpu.VMEM((KEYS, TILE), F32),
            pltpu.VMEM((PROMPT, TILE), BF16),
            pltpu.VMEM((PROMPT, HD), F32),
            pltpu.VMEM((PROMPT, HD), F32),
        ],
        cost_estimate=pl.CostEstimate(
            flops=16 * 10**9, bytes_accessed=8 * 2**20, transcendentals=5 * 10**6
        ),
        compiler_params=pltpu.CompilerParams(vmem_limit_bytes=40 * 2**20),
        name="forward",
    )(info, *rows, *keyvals)


def backward_kernel(
    info, os, qs, gs, ks, vs, kt, tops, deltas, dq_part,
    d0, d1, d2, d3,
    r0, r1, r2, r3,
    dk, dv, dq,
):
    y = info[0]
    z = info[1]
    length = info[2]
    dk[...] = jnp.zeros_like(dk)
    dv[...] = jnp.zeros_like(dv)

    def tile_step(tile, chunks, first_masked):
        at = aligned(tile * TILE, TILE)
        low_pos, query_pos = tile_positions(tile, z)

        @pl.when(low_pos < length)
        def _():
            q = qs[at, :]
            qt = q.T
            grad = gs[at, :]
            grad_t = grad.T
            stat = aligned(tile * 8, 8)
            top = tops[stat, :][:1]
            delta = deltas[stat, :][:1]
            dq_t = dq_part[aligned(tile * HD, HD), :]
            for c in range(chunks):
                rows = chunk_rows(c)
                s = jnp.dot(ks[rows, :], qt, preferred_element_type=F32)
                if c >= first_masked:
                    s = causal(s, c, query_pos)
                p = jnp.exp2((s - top) * SCALE2)
                dp = jnp.dot(vs[rows, :], grad_t, preferred_element_type=F32)
                ds = (p * (dp - delta)).astype(BF16)
                dv[rows, :] += jnp.dot(p.astype(BF16), grad, preferred_element_type=F32)
                dk[rows, :] += jnp.dot(ds, q, preferred_element_type=F32)
                dq_t = dq_t + jnp.dot(kt[:, rows], ds, preferred_element_type=F32)
            dq[at, :] = (dq_t * SCALE).T.astype(BF16)

        @pl.when(low_pos >= length)
        def _():
            dq[at, :] = jnp.zeros((TILE, HD), BF16)

    over_tiles(tile_step)
    for s, d in ((0, d0), (2, d2)):
        d[:GROUP, :] = os[head_rows(y + s), :]
        d[GROUP:, :] = dq[head_rows(y + s), :]
    d1[...] = dq[head_rows(y + 1), :]
    d3[...] = dq[head_rows(y + 3), :]
    for s, r in enumerate((r0, r1, r2, r3)):
        zp = lax.rem(z + s, NZ)
        for b in range(NY):
            at = aligned((b * NZ + zp) * BLOCK, BLOCK)
            r[b, 0] = (dk[at, :] * SCALE).astype(BF16)
            r[b, 1] = dv[at, :].astype(BF16)


def backward(info, state):
    return pl.pallas_call(
        backward_kernel,
        out_shape=[shaped((rows, HD), BF16) for rows in (2 * GROUP, GROUP, 2 * GROUP, GROUP)]
        + [shaped((NY, 2, BLOCK, HD), BF16)] * 4,
        in_specs=[SMEM] + [VMEM] * 9,
        out_specs=[VMEM] * 8,
        scratch_shapes=[
            pltpu.VMEM((RESP, HD), F32),
            pltpu.VMEM((RESP, HD), F32),
            pltpu.VMEM((ROWS, HD), BF16),
        ],
        cost_estimate=pl.CostEstimate(
            flops=16 * 10**9, bytes_accessed=8 * 2**20, transcendentals=5 * 10**6
        ),
        compiler_params=pltpu.CompilerParams(vmem_limit_bytes=40 * 2**20),
        name="backward",
    )(info, *state)


def lay_heads(y, pieces, out):
    for s, (piece, first) in enumerate(pieces):
        block = lax.rem(y - s + NY, NY)
        for j in range(HEADS):
            at = aligned((block * HEADS + j) * HD, HD)
            out[:, at] = piece[first + j * BLOCK : first + (j + 1) * BLOCK, :]


def settle_kernel(
    info, d0, d1, d2, d3, a1, a3, r0, r1, r2, r3, prompt, a, p0, p1, p2, p3
):
    y = info[0]
    lay_heads(y, ((d0, 0), (a1, 0), (d2, 0), (a3, 0)), a)
    for s, p in enumerate((p0, p1, p2, p3)):
        b = lax.rem(y + s, NY)
        for i in range(2):
            p[i * PIECE : i * PIECE + PROMPT_ROWS, :] = prompt[b, i].astype(BF16)
            p[i * PIECE + PROMPT_ROWS : (i + 1) * PIECE, :] = (
                (r0[b, i].astype(F32) + r1[b, i].astype(F32))
                + (r2[b, i].astype(F32) + r3[b, i].astype(F32))
            ).astype(BF16)
    p1[2 * PIECE :, :] = d1[...]
    p3[2 * PIECE :, :] = d3[...]


def settle(info, rows, att, terms, prompt):
    return pl.pallas_call(
        settle_kernel,
        out_shape=[shaped((BLOCK, NY * HEADS * HD), BF16)]
        + [shaped((2 * PIECE + s % 2 * GROUP, HD), BF16) for s in range(NY)],
        in_specs=[SMEM] + [VMEM] * 11,
        out_specs=[VMEM] * 5,
        name="settle",
    )(info, *rows, *att, *terms, prompt)


def place_kernel(info, d0, d2, p0, p1, p2, p3, d, dk, dv, pk, pv):
    y = info[0]
    lay_heads(y, ((d0, GROUP), (p1, 2 * PIECE), (d2, GROUP), (p3, 2 * PIECE)), d)
    for s, p in enumerate((p0, p1, p2, p3)):
        at = aligned(lax.rem(y - s + NY, NY) * HD, HD)
        pk[:, at] = p[:PROMPT_ROWS, :].astype(F32)
        dk[:, at] = p[PROMPT_ROWS:PIECE, :].astype(F32)
        pv[:, at] = p[PIECE : PIECE + PROMPT_ROWS, :].astype(F32)
        dv[:, at] = p[PIECE + PROMPT_ROWS : 2 * PIECE, :].astype(F32)


def place(info, rows, pieces):
    out = shaped((BLOCK, NY * HD), F32)
    prompt_out = shaped((PROMPT_ROWS, NY * HD), F32)
    return pl.pallas_call(
        place_kernel,
        out_shape=[shaped((BLOCK, NY * HEADS * HD), BF16), out, out, prompt_out, prompt_out],
        in_specs=[SMEM] + [VMEM] * 6,
        out_specs=[VMEM] * 5,
        name="place",
    )(info, *rows, *pieces)


def y_shift(a, s):
    pairs = [(i * NZ + k, (i + s) % NY * NZ + k) for i in range(NY) for k in range(NZ)]
    return lax.ppermute(a, "prefix", pairs)


def z_shift(a, s):
    pairs = [(i * NZ + k, i * NZ + (k + s) % NZ) for i in range(NY) for k in range(NZ)]
    return lax.ppermute(a, "prefix", pairs)


def core_swap(a):
    return lax.ppermute(a, "resp", [(i, i ^ 1) for i in range(16)])


def x_swap(a, bit):
    return lax.ppermute(a, "resp", [(i, i ^ (2 * bit)) for i in range(16)])


def far_swap(a):
    return lax.ppermute(a, "resp", [(i, i ^ 8) for i in range(16)])


def over_responses(terms):
    core = lax.axis_index("resp") % 2
    dk, dv = terms[0], terms[1]
    half = jnp.where(core == 0, dk, dv) + core_swap(jnp.where(core == 0, dv, dk))
    for swap in (lambda a: x_swap(a, 1), lambda a: x_swap(a, 2), far_swap):
        low = half.astype(BF16)
        half = low.astype(F32) + swap(low).astype(F32)
    other = core_swap(half.astype(BF16)).astype(F32)
    half = half.astype(BF16).astype(F32)
    return jnp.stack([jnp.where(core == 0, half, other), jnp.where(core == 0, other, half)])


def bring_rows(state):
    x1, x2, x3 = state
    x2 = y_shift(x2, 2)
    x3 = y_shift(x3, 3)
    x1, x3 = lax.optimization_barrier((x1, x3))
    return y_shift(x1, 1), x2, x3


def by_y(pieces):
    return [pieces[0]] + [y_shift(pieces[s], s) for s in range(1, NY)]


def by_z(pieces):
    return [pieces[0]] + [z_shift(pieces[s], s) for s in range(1, NZ)]


def per_device(
    response_queries,
    response_keys,
    response_values,
    prompt_keys,
    prompt_values,
    output_grad,
    lengths,
):
    prefix = lax.axis_index("prefix")
    y, z = prefix // NZ, prefix % NZ
    info = jnp.stack([y, z, lengths[lax.axis_index("resp")]]).astype(jnp.int32)
    pick = lax.dynamic_index_in_dim

    def split(a, width):
        return [
            lax.dynamic_slice_in_dim(a, (y + s) % NY * width, width, a.ndim - 1)
            for s in range(NY)
        ]

    prompt = by_z([jnp.stack([prompt_keys, prompt_values])] * NZ)
    keyvals = by_y(split(jnp.concatenate([response_keys, response_values]), HD))
    stacked = jnp.stack(keyvals)
    keyvals = jnp.stack([pick(stacked, (y - b) % NY, 0, keepdims=False) for b in range(NY)])
    keyvals, *prompt = lax.optimization_barrier((keyvals, *prompt))
    keyvals = by_z([keyvals] * NZ)
    x0, *rows = pack(info, response_queries[0], output_grad[0], prompt)
    once = jnp.minimum(lengths[0], 1)
    rows = lax.fori_loop(0, once, lambda i, state: bring_rows(state), tuple(rows))

    results = forward(info, (x0, *rows), keyvals)
    prompt_terms = by_z(results[:4])
    att = [y_shift(results[4], 1), y_shift(results[5], 3)]
    d0, d1, d2, d3, *terms = backward(info, results[6:])
    *prompt_terms, att[0], att[1], d2, terms[1], terms[2], terms[3] = lax.optimization_barrier(
        (*prompt_terms, *att, d2, terms[1], terms[2], terms[3])
    )
    prompt = sum(t.astype(F32) for t in prompt_terms)
    prompt = prompt.transpose(1, 0, 2, 3).reshape(2, NY * PROMPT_ROWS, HD)
    terms = by_z(terms)
    d2 = y_shift(d2, 2)
    prompt = lax.fori_loop(0, once, lambda i, terms: over_responses(terms), prompt)
    prompt = prompt.reshape(2, NY, PROMPT_ROWS, HD).transpose(1, 0, 2, 3)
    attention_out, *pieces = settle(info, (d0, d1, d2, d3), att, terms, prompt)
    query_grad, key_own, value_own, prompt_key_grad, prompt_value_grad = place(
        info, (d0, d2), by_y(pieces)
    )
    return (
        attention_out[None],
        query_grad[None],
        key_own[None],
        value_own[None],
        prompt_key_grad,
        prompt_value_grad,
    )


def solution(mesh):
    return jax.shard_map(
        per_device,
        mesh=mesh,
        in_specs=(
            P("resp", "prefix", None),
            P("resp", "prefix", None),
            P("resp", "prefix", None),
            P("prefix", None),
            P("prefix", None),
            P("resp", "prefix", None),
            P(),
        ),
        out_specs=(
            P("resp", "prefix", None),
            P("resp", "prefix", None),
            P("resp", "prefix", None),
            P("resp", "prefix", None),
            P("prefix", None),
            P("prefix", None),
        ),
        check_vma=False,
    )
```

```python
import math

import jax
import jax.numpy as jnp
from jax import lax
from jax.experimental import pallas as pl
from jax.experimental.pallas import tpu as pltpu
from jax.sharding import PartitionSpec as P

HD = 128
BLOCK = 128
PROMPT_ROWS = 48
PIECE = PROMPT_ROWS + BLOCK
HEADS = 5
NY = 4
NZ = 4
PROMPT = PROMPT_ROWS * NY * NZ
KEYS = PROMPT + BLOCK * NY * NZ
ROWS = NY * HEADS * BLOCK
CHUNK = 256
TILE = 256
MASKED = -1e30
SCALE = 1.0 / math.sqrt(HD)
SCALE2 = SCALE * math.log2(math.e)
F32 = jnp.float32
BF16 = jnp.bfloat16
CLASSES = ((0, 2, 2, 0), (2, 4, 4, 0), (4, 5, 4, 0), (5, 7, 6, 4), (7, 9, 8, 4), (9, 10, 8, 4))
TILES = ROWS // TILE
RESP = KEYS - PROMPT
GROUP = HEADS * BLOCK
VMEM = pl.BlockSpec(memory_space=pltpu.VMEM)
SMEM = pl.BlockSpec(memory_space=pltpu.SMEM)


def shaped(shape, dtype):
    return jax.ShapeDtypeStruct(shape, dtype)


def aligned(start, size):
    if isinstance(start, int):
        return slice(start, start + size)
    return pl.ds(pl.multiple_of(start, size), size)


def head_rows(block):
    return aligned(lax.rem(block, NY) * GROUP, GROUP)


def tile_positions(tile, z):
    u = tile * 2
    lane = lax.broadcasted_iota(jnp.int32, (1, TILE), 1)
    low = (u // HEADS * NZ + z) * BLOCK
    high = ((u + 1) // HEADS * NZ + z) * BLOCK - BLOCK
    return lane + jnp.where(lane < BLOCK, low, high)


def causal(s, chunks, first_masked, query_pos):
    end, start = chunks * CHUNK, first_masked * CHUNK
    key_pos = lax.broadcasted_iota(jnp.int32, (end - start, TILE), 0) + start
    last = jnp.where(key_pos <= query_pos, s[start:], MASKED)
    return jnp.concatenate([s[:start], last]) if start else last


def over_tiles(z, length, body, skip):
    for first, last, chunks, first_masked in CLASSES:
        low_pos = (first * 2 // HEADS * NZ + z) * BLOCK

        @pl.when(low_pos < length)
        def _(first=first, last=last, chunks=chunks, first_masked=first_masked):
            for tile in range(first, last):
                body(tile, chunks, first_masked)

        @pl.when(low_pos >= length)
        def _(first=first, last=last):
            skip(slice(first * TILE, last * TILE))


def forward_kernel(
    info,
    x0, x1, x2, x3,
    kv0, kv1, kv2, kv3,
    r0, r1, r2, r3,
    a1, a3, os, qs, gs, ks, vs, kt, tops, deltas, dq_part,
    kp, vp, kpt, vpt, vt, dk, dv,
):
    y = info[0]
    z = info[1]
    length = info[2]
    for s, x in enumerate((x0, x1, x2, x3)):
        block = lax.rem(y - s + NY, NY)
        start = (block * NZ + z) * BLOCK
        valid = (lax.broadcasted_iota(jnp.int32, (BLOCK, HD), 0) + start) < length
        for j in range(HEADS):
            at = aligned((block * HEADS + j) * BLOCK, BLOCK)
            cols = slice(j * HD, (j + 1) * HD)
            qs[at, :] = x[0, :, cols]
            gs[at, :] = jnp.where(valid, x[1, :, cols].astype(F32), 0.0).astype(BF16)
    for s, kv in enumerate((kv0, kv1, kv2, kv3)):
        zp = lax.rem(z - s + NZ, NZ)
        for b in range(NY):
            at = aligned((zp * NY + b) * PROMPT_ROWS, PROMPT_ROWS)
            kp[at, :] = kv[b, 0, :PROMPT_ROWS, :]
            vp[at, :] = kv[b, 1, :PROMPT_ROWS, :]
            at = aligned((b * NZ + zp) * BLOCK, BLOCK)
            k = kv[b, 0, PROMPT_ROWS:, :]
            v = kv[b, 1, PROMPT_ROWS:, :]
            ks[at, :] = k
            vs[at, :] = v
            kt[:, at] = k.T
            vt[:, at] = v.T
    for c in range(PROMPT // BLOCK):
        rows = slice(c * BLOCK, (c + 1) * BLOCK)
        kpt[:, rows] = kp[rows, :].T
        vpt[:, rows] = vp[rows, :].T
    dk[...] = jnp.zeros_like(dk)
    dv[...] = jnp.zeros_like(dv)

    def tile_step(tile, chunks, first_masked):
        at = aligned(tile * TILE, TILE)
        query_pos = tile_positions(tile, z)
        q = qs[at, :]
        qt = q.T
        n = chunks * CHUNK
        first = jnp.dot(kp[...], qt, preferred_element_type=F32)
        s = jnp.dot(ks[:n, :], qt, preferred_element_type=F32)
        s = causal(s, chunks, first_masked, query_pos)
        top = jnp.maximum(jnp.max(first, axis=0, keepdims=True), jnp.max(s, axis=0, keepdims=True))
        p = jnp.exp2((first - top) * SCALE2)
        total = jnp.sum(p, axis=0, keepdims=True)
        low = p.astype(BF16)
        out_t = jnp.dot(vpt[...], low, preferred_element_type=F32)
        p = jnp.exp2((s - top) * SCALE2)
        total = total + jnp.sum(p, axis=0, keepdims=True)
        out_t = out_t + jnp.dot(vt[:, :n], p.astype(BF16), preferred_element_type=F32)
        inv = 1.0 / jnp.sum(total, axis=0, keepdims=True)
        out_t = out_t * inv
        os[at, :] = jnp.where(query_pos < length, out_t, 0.0).T.astype(BF16)
        grad_t = gs[at, :].astype(F32).T
        delta = jnp.sum(grad_t * out_t, axis=0, keepdims=True) * inv
        grad_t = grad_t * inv
        grad = grad_t.T.astype(BF16)
        grad_t = grad_t.astype(BF16)
        gs[at, :] = grad
        stat = aligned(tile * 8, 8)
        tops[stat, :] = jnp.broadcast_to(top, (8, TILE))
        deltas[stat, :] = jnp.broadcast_to(delta, (8, TILE))
        dq_t = jnp.zeros((HD, TILE), F32)
        dp = jnp.dot(vp[...], grad_t, preferred_element_type=F32)
        ds = (low.astype(F32) * (dp - delta)).astype(BF16)
        dv[...] += jnp.dot(low, grad, preferred_element_type=F32)
        dk[...] += jnp.dot(ds, q, preferred_element_type=F32)
        dq_t = dq_t + jnp.dot(kpt[...], ds, preferred_element_type=F32)
        dq_part[aligned(tile * HD, HD), :] = dq_t

    def skip(rows):
        os[rows, :] = jnp.zeros((rows.stop - rows.start, HD), BF16)

    over_tiles(z, length, tile_step, skip)
    a1[...] = os[head_rows(y + 1), :]
    a3[...] = os[head_rows(y + 3), :]
    for s, r in enumerate((r0, r1, r2, r3)):
        zp = lax.rem(z + s, NZ)
        for b in range(NY):
            at = aligned((zp * NY + b) * PROMPT_ROWS, PROMPT_ROWS)
            r[b, 0] = (dk[at, :] * SCALE).astype(BF16)
            r[b, 1] = dv[at, :].astype(BF16)


def forward(info, rows, keyvals):
    return pl.pallas_call(
        forward_kernel,
        out_shape=[shaped((NY, 2, PROMPT_ROWS, HD), BF16)] * 4
        + [shaped((GROUP, HD), BF16)] * 2
        + [
            shaped((ROWS, HD), BF16),
            shaped((ROWS, HD), BF16),
            shaped((ROWS, HD), BF16),
            shaped((RESP, HD), BF16),
            shaped((RESP, HD), BF16),
            shaped((HD, RESP), BF16),
            shaped((TILES * 8, TILE), F32),
            shaped((TILES * 8, TILE), F32),
            shaped((TILES * HD, TILE), F32),
        ],
        in_specs=[SMEM] + [VMEM] * 8,
        out_specs=[VMEM] * 15,
        scratch_shapes=[
            pltpu.VMEM((PROMPT, HD), BF16),
            pltpu.VMEM((PROMPT, HD), BF16),
            pltpu.VMEM((HD, PROMPT), BF16),
            pltpu.VMEM((HD, PROMPT), BF16),
            pltpu.VMEM((HD, RESP), BF16),
            pltpu.VMEM((PROMPT, HD), F32),
            pltpu.VMEM((PROMPT, HD), F32),
        ],
        cost_estimate=pl.CostEstimate(
            flops=16 * 10**9, bytes_accessed=8 * 2**20, transcendentals=5 * 10**6
        ),
        compiler_params=pltpu.CompilerParams(vmem_limit_bytes=40 * 2**20),
        name="forward",
    )(info, *rows, *keyvals)


def backward_kernel(
    info, os, qs, gs, ks, vs, kt, tops, deltas, dq_part,
    d0, d1, d2, d3,
    r0, r1, r2, r3,
    dk, dv, dq,
):
    y = info[0]
    z = info[1]
    length = info[2]
    dk[...] = jnp.zeros_like(dk)
    dv[...] = jnp.zeros_like(dv)

    def tile_step(tile, chunks, first_masked):
        at = aligned(tile * TILE, TILE)
        query_pos = tile_positions(tile, z)
        q = qs[at, :]
        qt = q.T
        grad = gs[at, :]
        grad_t = grad.T
        stat = aligned(tile * 8, 8)
        top = tops[stat, :][:1]
        delta = deltas[stat, :][:1]
        dq_t = dq_part[aligned(tile * HD, HD), :]
        n = chunks * CHUNK
        s = jnp.dot(ks[:n, :], qt, preferred_element_type=F32)
        s = causal(s, chunks, first_masked, query_pos)
        p = jnp.exp2((s - top) * SCALE2)
        dp = jnp.dot(vs[:n, :], grad_t, preferred_element_type=F32)
        ds = (p * (dp - delta)).astype(BF16)
        dv[:n, :] += jnp.dot(p.astype(BF16), grad, preferred_element_type=F32)
        dk[:n, :] += jnp.dot(ds, q, preferred_element_type=F32)
        dq_t = dq_t + jnp.dot(kt[:, :n], ds, preferred_element_type=F32)
        dq[at, :] = (dq_t * SCALE).T.astype(BF16)

    def skip(rows):
        dq[rows, :] = jnp.zeros((rows.stop - rows.start, HD), BF16)

    over_tiles(z, length, tile_step, skip)
    for s, d in ((0, d0), (2, d2)):
        d[:GROUP, :] = os[head_rows(y + s), :]
        d[GROUP:, :] = dq[head_rows(y + s), :]
    d1[...] = dq[head_rows(y + 1), :]
    d3[...] = dq[head_rows(y + 3), :]
    for s, r in enumerate((r0, r1, r2, r3)):
        zp = lax.rem(z + s, NZ)
        for b in range(NY):
            at = aligned((b * NZ + zp) * BLOCK, BLOCK)
            r[b, 0] = (dk[at, :] * SCALE).astype(BF16)
            r[b, 1] = dv[at, :].astype(BF16)


def backward(info, state):
    return pl.pallas_call(
        backward_kernel,
        out_shape=[shaped((rows, HD), BF16) for rows in (2 * GROUP, GROUP, 2 * GROUP, GROUP)]
        + [shaped((NY, 2, BLOCK, HD), BF16)] * 4,
        in_specs=[SMEM] + [VMEM] * 9,
        out_specs=[VMEM] * 8,
        scratch_shapes=[
            pltpu.VMEM((RESP, HD), F32),
            pltpu.VMEM((RESP, HD), F32),
            pltpu.VMEM((ROWS, HD), BF16),
        ],
        cost_estimate=pl.CostEstimate(
            flops=16 * 10**9, bytes_accessed=8 * 2**20, transcendentals=5 * 10**6
        ),
        compiler_params=pltpu.CompilerParams(vmem_limit_bytes=40 * 2**20),
        name="backward",
    )(info, *state)


def lay_heads(y, pieces, out):
    for s, (piece, first) in enumerate(pieces):
        block = lax.rem(y - s + NY, NY)
        for j in range(HEADS):
            at = aligned((block * HEADS + j) * HD, HD)
            out[:, at] = piece[first + j * BLOCK : first + (j + 1) * BLOCK, :]


def settle_kernel(
    info, d1, d3, r0, r1, r2, r3, prompt, p0, p1, p2, p3
):
    y = info[0]
    for s, p in enumerate((p0, p1, p2, p3)):
        b = lax.rem(y + s, NY)
        for i in range(2):
            p[i * PIECE : i * PIECE + PROMPT_ROWS, :] = prompt[b, i].astype(BF16)
            p[i * PIECE + PROMPT_ROWS : (i + 1) * PIECE, :] = (
                (r0[b, i].astype(F32) + r1[b, i].astype(F32))
                + (r2[b, i].astype(F32) + r3[b, i].astype(F32))
            ).astype(BF16)
    p1[2 * PIECE :, :] = d1[...]
    p3[2 * PIECE :, :] = d3[...]


def settle(info, rows, terms, prompt):
    return pl.pallas_call(
        settle_kernel,
        out_shape=[shaped((2 * PIECE + s % 2 * GROUP, HD), BF16) for s in range(NY)],
        in_specs=[SMEM] + [VMEM] * 7,
        out_specs=[VMEM] * 4,
        compiler_params=pltpu.CompilerParams(vmem_limit_bytes=16 * 2**20),
        name="settle",
    )(info, *rows, *terms, prompt)


def attention_kernel(info, d0, a1, d2, a3, out):
    lay_heads(info[0], ((d0, 0), (a1, 0), (d2, 0), (a3, 0)), out)


def lay_attention(info, pieces):
    return pl.pallas_call(
        attention_kernel,
        out_shape=shaped((BLOCK, NY * HEADS * HD), BF16),
        in_specs=[SMEM] + [VMEM] * 4,
        out_specs=VMEM,
        compiler_params=pltpu.CompilerParams(vmem_limit_bytes=16 * 2**20),
        name="lay_attention",
    )(info, *pieces)


def place_kernel(info, done, d0, d2, p0, p1, p2, p3, d, dk, dv, pk, pv):
    y = info[0]
    lay_heads(y, ((d0, GROUP), (p1, 2 * PIECE), (d2, GROUP), (p3, 2 * PIECE)), d)
    for s, p in enumerate((p0, p1, p2, p3)):
        at = aligned(lax.rem(y - s + NY, NY) * HD, HD)
        pk[:, at] = p[:PROMPT_ROWS, :].astype(F32)
        dk[:, at] = p[PROMPT_ROWS:PIECE, :].astype(F32)
        pv[:, at] = p[PIECE : PIECE + PROMPT_ROWS, :].astype(F32)
        dv[:, at] = p[PIECE + PROMPT_ROWS : 2 * PIECE, :].astype(F32)


def place(info, done, rows, pieces):
    out = shaped((BLOCK, NY * HD), F32)
    prompt_out = shaped((PROMPT_ROWS, NY * HD), F32)
    return pl.pallas_call(
        place_kernel,
        out_shape=[shaped((BLOCK, NY * HEADS * HD), BF16), out, out, prompt_out, prompt_out],
        in_specs=[SMEM, pl.BlockSpec(memory_space=pl.ANY)] + [VMEM] * 6,
        out_specs=[VMEM] * 5,
        compiler_params=pltpu.CompilerParams(vmem_limit_bytes=16 * 2**20),
        name="place",
    )(info, done, *rows, *pieces)


def y_shift(a, s):
    pairs = [(i * NZ + k, (i + s) % NY * NZ + k) for i in range(NY) for k in range(NZ)]
    return lax.ppermute(a, "prefix", pairs)


def z_shift(a, s):
    pairs = [(i * NZ + k, i * NZ + (k + s) % NZ) for i in range(NY) for k in range(NZ)]
    return lax.ppermute(a, "prefix", pairs)


def core_swap(a):
    return lax.ppermute(a, "resp", [(i, i ^ 1) for i in range(16)])


def x_swap(a, bit):
    return lax.ppermute(a, "resp", [(i, i ^ (2 * bit)) for i in range(16)])


def far_swap(a):
    return lax.ppermute(a, "resp", [(i, i ^ 8) for i in range(16)])


def over_responses(terms):
    core = lax.axis_index("resp") % 2
    dk, dv = terms[0], terms[1]
    half = jnp.where(core == 0, dk, dv) + core_swap(jnp.where(core == 0, dv, dk))
    for swap in (lambda a: x_swap(a, 1), lambda a: x_swap(a, 2), far_swap):
        low = half.astype(BF16)
        half = low.astype(F32) + swap(low).astype(F32)
    other = core_swap(half.astype(BF16)).astype(F32)
    half = half.astype(BF16).astype(F32)
    return jnp.stack([jnp.where(core == 0, half, other), jnp.where(core == 0, other, half)])


def by_y(pieces):
    return [pieces[0]] + [y_shift(pieces[s], s) for s in range(1, NY)]


def by_z(pieces):
    return [pieces[0]] + [z_shift(pieces[s], s) for s in range(1, NZ)]


def per_device(
    response_queries,
    response_keys,
    response_values,
    prompt_keys,
    prompt_values,
    output_grad,
    lengths,
):
    prefix = lax.axis_index("prefix")
    y, z = prefix // NZ, prefix % NZ
    info = jnp.stack([y, z, lengths[lax.axis_index("resp")]]).astype(jnp.int32)
    pick = lax.dynamic_index_in_dim

    def split(a, width):
        return [
            lax.dynamic_slice_in_dim(a, (y + s) % NY * width, width, a.ndim - 1)
            for s in range(NY)
        ]

    keyvals = jnp.stack(
        [
            jnp.concatenate([prompt_keys, response_keys[0]], axis=0),
            jnp.concatenate([prompt_values, response_values[0]], axis=0),
        ]
    )
    keyvals = by_y(split(keyvals, HD))
    *keyvals, queries, grads = lax.optimization_barrier(
        (*keyvals, response_queries[0], output_grad[0])
    )
    stacked = jnp.stack(keyvals)
    keyvals = jnp.stack([pick(stacked, (y - b) % NY, 0, keepdims=False) for b in range(NY)])
    keyvals = by_z([keyvals] * NZ)
    rows = by_y(split(jnp.stack([queries, grads]), HEADS * HD))

    results = forward(info, rows, keyvals)
    prompt_terms = by_z(results[:4])
    att = [y_shift(results[4], 1), y_shift(results[5], 3)]
    d0, d1, d2, d3, *terms = backward(info, results[6:])
    *prompt_terms, att[0], att[1], d2, terms[1], terms[2], terms[3] = lax.optimization_barrier(
        (*prompt_terms, *att, d2, terms[1], terms[2], terms[3])
    )
    prompt = sum(t.astype(F32) for t in prompt_terms)
    prompt = prompt.transpose(1, 0, 2, 3).reshape(2, NY * PROMPT_ROWS, HD)
    once = jnp.minimum(lengths[0], 1)
    terms = by_z(terms)
    d2 = y_shift(d2, 2)
    prompt = lax.fori_loop(0, once, lambda i, terms: over_responses(terms), prompt)
    prompt = prompt.reshape(2, NY, PROMPT_ROWS, HD).transpose(1, 0, 2, 3)
    pieces = settle(info, (d1, d3), terms, prompt)
    d2, *pieces = lax.optimization_barrier((d2, *pieces))
    attention_out = lay_attention(info, (d0, att[0], d2, att[1]))
    query_grad, key_own, value_own, prompt_key_grad, prompt_value_grad = place(
        info, attention_out, (d0, d2), by_y(pieces)
    )
    return (
        attention_out[None],
        query_grad[None],
        key_own[None],
        value_own[None],
        prompt_key_grad,
        prompt_value_grad,
    )


def solution(mesh):
    return jax.shard_map(
        per_device,
        mesh=mesh,
        in_specs=(
            P("resp", "prefix", None),
            P("resp", "prefix", None),
            P("resp", "prefix", None),
            P("prefix", None),
            P("prefix", None),
            P("resp", "prefix", None),
            P(),
        ),
        out_specs=(
            P("resp", "prefix", None),
            P("resp", "prefix", None),
            P("resp", "prefix", None),
            P("resp", "prefix", None),
            P("prefix", None),
            P("prefix", None),
        ),
        check_vma=False,
    )
```

```python
import math

import jax
import jax.numpy as jnp
from jax import lax
from jax.experimental import pallas as pl
from jax.experimental.pallas import tpu as pltpu
from jax.sharding import PartitionSpec as P

HD = 128
BLOCK = 128
PROMPT_ROWS = 48
PIECE = PROMPT_ROWS + BLOCK
HEADS = 5
NY = 4
NZ = 4
PROMPT = PROMPT_ROWS * NY * NZ
KEYS = PROMPT + BLOCK * NY * NZ
ROWS = NY * HEADS * BLOCK
CHUNK = 256
TILE = 256
MASKED = -1e30
SCALE = 1.0 / math.sqrt(HD)
SCALE2 = SCALE * math.log2(math.e)
F32 = jnp.float32
BF16 = jnp.bfloat16
CLASSES = ((0, 2, 2, 0), (2, 4, 4, 0), (4, 5, 4, 0), (5, 7, 6, 4), (7, 9, 8, 4), (9, 10, 8, 4))
TILES = ROWS // TILE
RESP = KEYS - PROMPT
GROUP = HEADS * BLOCK
VMEM = pl.BlockSpec(memory_space=pltpu.VMEM)
SMEM = pl.BlockSpec(memory_space=pltpu.SMEM)


def shaped(shape, dtype):
    return jax.ShapeDtypeStruct(shape, dtype)


def aligned(start, size):
    if isinstance(start, int):
        return slice(start, start + size)
    return pl.ds(pl.multiple_of(start, size), size)


def head_rows(block):
    return aligned(lax.rem(block, NY) * GROUP, GROUP)


def tile_positions(tile, z):
    u = tile * 2
    lane = lax.broadcasted_iota(jnp.int32, (1, TILE), 1)
    low = (u // HEADS * NZ + z) * BLOCK
    high = ((u + 1) // HEADS * NZ + z) * BLOCK - BLOCK
    return lane + jnp.where(lane < BLOCK, low, high)


def causal(s, chunks, first_masked, query_pos):
    end, start = chunks * CHUNK, first_masked * CHUNK
    key_pos = lax.broadcasted_iota(jnp.int32, (end - start, TILE), 0) + start
    last = jnp.where(key_pos <= query_pos, s[start:], MASKED)
    return jnp.concatenate([s[:start], last]) if start else last


def over_tiles(z, length, body, skip):
    for first, last, chunks, first_masked in CLASSES:
        low_pos = (first * 2 // HEADS * NZ + z) * BLOCK

        @pl.when(low_pos < length)
        def _(first=first, last=last, chunks=chunks, first_masked=first_masked):
            for tile in range(first, last):
                body(tile, chunks, first_masked)

        @pl.when(low_pos >= length)
        def _(first=first, last=last):
            skip(slice(first * TILE, last * TILE))


def attend_kernel(
    info,
    x0, x1, x2, x3,
    kv0, kv1, kv2, kv3,
    p0, p1, p2, p3,
    d0, d1, d2, d3,
    r0, r1, r2, r3,
    qs, gs, ks, vs, kt, vt, kp, vp, kpt, vpt, dk, dv, dkp, dvp, os, dq,
):
    y = info[0]
    z = info[1]
    length = info[2]
    for s, x in enumerate((x0, x1, x2, x3)):
        block = lax.rem(y - s + NY, NY)
        start = (block * NZ + z) * BLOCK
        valid = (lax.broadcasted_iota(jnp.int32, (BLOCK, HD), 0) + start) < length
        for j in range(HEADS):
            at = aligned((block * HEADS + j) * BLOCK, BLOCK)
            cols = slice(j * HD, (j + 1) * HD)
            qs[at, :] = x[0, :, cols]
            gs[at, :] = jnp.where(valid, x[1, :, cols].astype(F32), 0.0).astype(BF16)
    for s, kv in enumerate((kv0, kv1, kv2, kv3)):
        zp = lax.rem(z - s + NZ, NZ)
        for b in range(NY):
            at = aligned((zp * NY + b) * PROMPT_ROWS, PROMPT_ROWS)
            kp[at, :] = kv[b, 0, :PROMPT_ROWS, :]
            vp[at, :] = kv[b, 1, :PROMPT_ROWS, :]
            at = aligned((b * NZ + zp) * BLOCK, BLOCK)
            k = kv[b, 0, PROMPT_ROWS:, :]
            v = kv[b, 1, PROMPT_ROWS:, :]
            ks[at, :] = k
            vs[at, :] = v
            kt[:, at] = k.T
            vt[:, at] = v.T
    for c in range(PROMPT // BLOCK):
        rows = slice(c * BLOCK, (c + 1) * BLOCK)
        kpt[:, rows] = kp[rows, :].T
        vpt[:, rows] = vp[rows, :].T
    for grad in (dk, dv, dkp, dvp):
        grad[...] = jnp.zeros_like(grad)

    def tile_step(tile, chunks, first_masked):
        at = aligned(tile * TILE, TILE)
        query_pos = tile_positions(tile, z)
        q = qs[at, :]
        qt = q.T
        n = chunks * CHUNK
        first = jnp.dot(kp[...], qt, preferred_element_type=F32)
        s = jnp.dot(ks[:n, :], qt, preferred_element_type=F32)
        s = causal(s, chunks, first_masked, query_pos)
        top = jnp.maximum(
            jnp.max(first, axis=0, keepdims=True), jnp.max(s, axis=0, keepdims=True)
        )
        first = jnp.exp2((first - top) * SCALE2)
        total = jnp.sum(first, axis=0, keepdims=True)
        first = first.astype(BF16)
        out_t = jnp.dot(vpt[...], first, preferred_element_type=F32)
        p = jnp.exp2((s - top) * SCALE2)
        total = total + jnp.sum(p, axis=0, keepdims=True)
        p = p.astype(BF16)
        out_t = out_t + jnp.dot(vt[:, :n], p, preferred_element_type=F32)
        inv = 1.0 / total
        out_t = out_t * inv
        os[at, :] = jnp.where(query_pos < length, out_t, 0.0).T.astype(BF16)
        grad_t = gs[at, :].astype(F32).T
        delta = jnp.sum(grad_t * out_t, axis=0, keepdims=True) * inv
        grad_t = grad_t * inv
        grad = grad_t.T.astype(BF16)
        grad_t = grad_t.astype(BF16)
        dp = jnp.dot(vp[...], grad_t, preferred_element_type=F32)
        ds = (first.astype(F32) * (dp - delta)).astype(BF16)
        dvp[...] += jnp.dot(first, grad, preferred_element_type=F32)
        dkp[...] += jnp.dot(ds, q, preferred_element_type=F32)
        dq_t = jnp.dot(kpt[...], ds, preferred_element_type=F32)
        dp = jnp.dot(vs[:n, :], grad_t, preferred_element_type=F32)
        ds = (p.astype(F32) * (dp - delta)).astype(BF16)
        dv[:n, :] += jnp.dot(p, grad, preferred_element_type=F32)
        dk[:n, :] += jnp.dot(ds, q, preferred_element_type=F32)
        dq_t = dq_t + jnp.dot(kt[:, :n], ds, preferred_element_type=F32)
        dq[at, :] = (dq_t * SCALE).T.astype(BF16)

    def skip(rows):
        os[rows, :] = jnp.zeros((rows.stop - rows.start, HD), BF16)
        dq[rows, :] = jnp.zeros((rows.stop - rows.start, HD), BF16)

    over_tiles(z, length, tile_step, skip)
    for s, d in enumerate((d0, d1, d2, d3)):
        d[:GROUP, :] = os[head_rows(y + s), :]
        d[GROUP:, :] = dq[head_rows(y + s), :]
    for s, (p, r) in enumerate(((p0, r0), (p1, r1), (p2, r2), (p3, r3))):
        zp = lax.rem(z + s, NZ)
        for b in range(NY):
            at = aligned((zp * NY + b) * PROMPT_ROWS, PROMPT_ROWS)
            p[b, 0] = (dkp[at, :] * SCALE).astype(BF16)
            p[b, 1] = dvp[at, :].astype(BF16)
            at = aligned((b * NZ + zp) * BLOCK, BLOCK)
            r[b, 0] = (dk[at, :] * SCALE).astype(BF16)
            r[b, 1] = dv[at, :].astype(BF16)


def attend(info, rows, keyvals):
    return pl.pallas_call(
        attend_kernel,
        out_shape=[shaped((NY, 2, PROMPT_ROWS, HD), BF16)] * NZ
        + [shaped((2 * GROUP, HD), BF16)] * NY
        + [shaped((NY, 2, BLOCK, HD), BF16)] * NZ,
        in_specs=[SMEM] + [VMEM] * 8,
        out_specs=[VMEM] * 12,
        scratch_shapes=[pltpu.VMEM((ROWS, HD), BF16)] * 2
        + [pltpu.VMEM((RESP, HD), BF16)] * 2
        + [pltpu.VMEM((HD, RESP), BF16)] * 2
        + [pltpu.VMEM((PROMPT, HD), BF16)] * 2
        + [pltpu.VMEM((HD, PROMPT), BF16)] * 2
        + [pltpu.VMEM((RESP, HD), F32)] * 2
        + [pltpu.VMEM((PROMPT, HD), F32)] * 2
        + [pltpu.VMEM((ROWS, HD), BF16)] * 2,
        compiler_params=pltpu.CompilerParams(vmem_limit_bytes=48 * 2**20),
        name="attend",
    )(info, *rows, *keyvals)


def settle_kernel(
    info, r0, r1, r2, r3, prompt, p0, p1, p2, p3
):
    y = info[0]
    for s, p in enumerate((p0, p1, p2, p3)):
        b = lax.rem(y + s, NY)
        for i in range(2):
            p[i * PIECE : i * PIECE + PROMPT_ROWS, :] = prompt[b, i].astype(BF16)
            p[i * PIECE + PROMPT_ROWS : (i + 1) * PIECE, :] = (
                (r0[b, i].astype(F32) + r1[b, i].astype(F32))
                + (r2[b, i].astype(F32) + r3[b, i].astype(F32))
            ).astype(BF16)


def settle(info, terms, prompt):
    return pl.pallas_call(
        settle_kernel,
        out_shape=[shaped((2 * PIECE, HD), BF16)] * NY,
        in_specs=[SMEM] + [VMEM] * 5,
        out_specs=[VMEM] * 4,
        compiler_params=pltpu.CompilerParams(vmem_limit_bytes=16 * 2**20),
        name="settle",
    )(info, *terms, prompt)


def rows_kernel(info, d0, d1, d2, d3, att, dq):
    y = info[0]
    for s, d in enumerate((d0, d1, d2, d3)):
        block = lax.rem(y - s + NY, NY)
        for j in range(HEADS):
            at = aligned((block * HEADS + j) * HD, HD)
            att[:, at] = d[j * BLOCK : (j + 1) * BLOCK, :]
            dq[:, at] = d[GROUP + j * BLOCK : GROUP + (j + 1) * BLOCK, :]


def lay_rows(info, pieces):
    return pl.pallas_call(
        rows_kernel,
        out_shape=[shaped((BLOCK, NY * HEADS * HD), BF16)] * 2,
        in_specs=[SMEM] + [VMEM] * 4,
        out_specs=[VMEM] * 2,
        compiler_params=pltpu.CompilerParams(vmem_limit_bytes=16 * 2**20),
        name="lay_rows",
    )(info, *pieces)


def place_kernel(info, done, p0, p1, p2, p3, dk, dv, pk, pv):
    y = info[0]
    for s, p in enumerate((p0, p1, p2, p3)):
        at = aligned(lax.rem(y - s + NY, NY) * HD, HD)
        pk[:, at] = p[:PROMPT_ROWS, :].astype(F32)
        dk[:, at] = p[PROMPT_ROWS:PIECE, :].astype(F32)
        pv[:, at] = p[PIECE : PIECE + PROMPT_ROWS, :].astype(F32)
        dv[:, at] = p[PIECE + PROMPT_ROWS : 2 * PIECE, :].astype(F32)


def place(info, done, pieces):
    out = shaped((BLOCK, NY * HD), F32)
    prompt_out = shaped((PROMPT_ROWS, NY * HD), F32)
    return pl.pallas_call(
        place_kernel,
        out_shape=[out, out, prompt_out, prompt_out],
        in_specs=[SMEM, pl.BlockSpec(memory_space=pl.ANY)] + [VMEM] * 4,
        out_specs=[VMEM] * 4,
        compiler_params=pltpu.CompilerParams(vmem_limit_bytes=16 * 2**20),
        name="place",
    )(info, done, *pieces)


def y_shift(a, s):
    pairs = [(i * NZ + k, (i + s) % NY * NZ + k) for i in range(NY) for k in range(NZ)]
    return lax.ppermute(a, "prefix", pairs)


def z_shift(a, s):
    pairs = [(i * NZ + k, i * NZ + (k + s) % NZ) for i in range(NY) for k in range(NZ)]
    return lax.ppermute(a, "prefix", pairs)


def core_swap(a):
    return lax.ppermute(a, "resp", [(i, i ^ 1) for i in range(16)])


def x_swap(a, bit):
    return lax.ppermute(a, "resp", [(i, i ^ (2 * bit)) for i in range(16)])


def far_swap(a):
    return lax.ppermute(a, "resp", [(i, i ^ 8) for i in range(16)])


def over_responses(terms):
    core = lax.axis_index("resp") % 2
    dk, dv = terms[0], terms[1]
    half = jnp.where(core == 0, dk, dv) + core_swap(jnp.where(core == 0, dv, dk))
    for swap in (lambda a: x_swap(a, 1), lambda a: x_swap(a, 2), far_swap):
        low = half.astype(BF16)
        half = low.astype(F32) + swap(low).astype(F32)
    other = core_swap(half.astype(BF16)).astype(F32)
    half = half.astype(BF16).astype(F32)
    return jnp.stack([jnp.where(core == 0, half, other), jnp.where(core == 0, other, half)])


def by_y(pieces):
    return [pieces[0]] + [y_shift(pieces[s], s) for s in range(1, NY)]


def by_z(pieces):
    return [pieces[0]] + [z_shift(pieces[s], s) for s in range(1, NZ)]


def per_device(
    response_queries,
    response_keys,
    response_values,
    prompt_keys,
    prompt_values,
    output_grad,
    lengths,
):
    prefix = lax.axis_index("prefix")
    y, z = prefix // NZ, prefix % NZ
    info = jnp.stack([y, z, lengths[lax.axis_index("resp")]]).astype(jnp.int32)
    pick = lax.dynamic_index_in_dim

    def split(a, width):
        return [
            lax.dynamic_slice_in_dim(a, (y + s) % NY * width, width, a.ndim - 1)
            for s in range(NY)
        ]

    keyvals = jnp.stack(
        [
            jnp.concatenate([prompt_keys, response_keys[0]], axis=0),
            jnp.concatenate([prompt_values, response_values[0]], axis=0),
        ]
    )
    keyvals = by_y(split(keyvals, HD))
    *keyvals, queries, grads = lax.optimization_barrier(
        (*keyvals, response_queries[0], output_grad[0])
    )
    stacked = jnp.stack(keyvals)
    keyvals = jnp.stack([pick(stacked, (y - b) % NY, 0, keepdims=False) for b in range(NY)])
    keyvals = by_z([keyvals] * NZ)
    rows = by_y(split(jnp.stack([queries, grads]), HEADS * HD))

    results = attend(info, rows, keyvals)
    prompt_terms = by_z(results[:4])
    d0, d1, d2, d3 = results[4:8]
    d1, d3 = y_shift(d1, 1), y_shift(d3, 3)
    *prompt_terms, d1, d3, d2, t1, t2, t3 = lax.optimization_barrier(
        (*prompt_terms, d1, d3, d2, *results[9:])
    )
    prompt = sum(t.astype(F32) for t in prompt_terms)
    prompt = prompt.transpose(1, 0, 2, 3).reshape(2, NY * PROMPT_ROWS, HD)
    once = jnp.minimum(lengths[0], 1)
    terms = by_z([results[8], t1, t2, t3])
    d2 = y_shift(d2, 2)
    prompt = lax.fori_loop(0, once, lambda i, terms: over_responses(terms), prompt)
    prompt = prompt.reshape(2, NY, PROMPT_ROWS, HD).transpose(1, 0, 2, 3)
    pieces = settle(info, terms, prompt)
    d2, *pieces = lax.optimization_barrier((d2, *pieces))
    attention_out, query_grad = lay_rows(info, (d0, d1, d2, d3))
    key_own, value_own, prompt_key_grad, prompt_value_grad = place(
        info, query_grad, by_y(pieces)
    )
    return (
        attention_out[None],
        query_grad[None],
        key_own[None],
        value_own[None],
        prompt_key_grad,
        prompt_value_grad,
    )


def solution(mesh):
    return jax.shard_map(
        per_device,
        mesh=mesh,
        in_specs=(
            P("resp", "prefix", None),
            P("resp", "prefix", None),
            P("resp", "prefix", None),
            P("prefix", None),
            P("prefix", None),
            P("resp", "prefix", None),
            P(),
        ),
        out_specs=(
            P("resp", "prefix", None),
            P("resp", "prefix", None),
            P("resp", "prefix", None),
            P("resp", "prefix", None),
            P("prefix", None),
            P("prefix", None),
        ),
        check_vma=False,
    )
```

```python
import math

import jax
import jax.numpy as jnp
from jax import lax
from jax.experimental import pallas as pl
from jax.experimental.pallas import tpu as pltpu
from jax.sharding import PartitionSpec as P

HD = 128
BLOCK = 128
PROMPT_ROWS = 48
PIECE = PROMPT_ROWS + BLOCK
HEADS = 5
NY = 4
NZ = 4
PROMPT = PROMPT_ROWS * NY * NZ
KEYS = PROMPT + BLOCK * NY * NZ
ROWS = NY * HEADS * BLOCK
CHUNK = 256
TILE = 256
MASKED = -1e30
SCALE = 1.0 / math.sqrt(HD)
SCALE2 = SCALE * math.log2(math.e)
F32 = jnp.float32
BF16 = jnp.bfloat16
CLASSES = ((0, 2, 2, 0), (2, 5, 4, 0), (5, 7, 6, 4), (7, 10, 8, 4))
TILES = ROWS // TILE
RESP = KEYS - PROMPT
GROUP = HEADS * BLOCK
VMEM = pl.BlockSpec(memory_space=pltpu.VMEM)
SMEM = pl.BlockSpec(memory_space=pltpu.SMEM)


def shaped(shape, dtype):
    return jax.ShapeDtypeStruct(shape, dtype)


def aligned(start, size):
    return pl.ds(pl.multiple_of(start, size), size)


def head_rows(block):
    return aligned(lax.rem(block, NY) * GROUP, GROUP)


def tile_positions(tile, z):
    u = tile * 2
    lane = lax.broadcasted_iota(jnp.int32, (1, TILE), 1)
    low = (u // HEADS * NZ + z) * BLOCK
    high = ((u + 1) // HEADS * NZ + z) * BLOCK - BLOCK
    return lane + jnp.where(lane < BLOCK, low, high)


def causal(s, chunks, first_masked, query_pos):
    end, start = chunks * CHUNK, first_masked * CHUNK
    key_pos = lax.broadcasted_iota(jnp.int32, (end - start, TILE), 0) + start
    last = jnp.where(key_pos <= query_pos, s[start:], MASKED)
    return jnp.concatenate([s[:start], last]) if start else last


def over_tiles(z, length, body, skip):
    for first, last, chunks, first_masked in CLASSES:

        def step(tile, carry, chunks=chunks, first_masked=first_masked):
            active = (tile * 2 // HEADS * NZ + z) * BLOCK < length

            @pl.when(active)
            def _():
                body(tile, chunks, first_masked)

            @pl.when(jnp.logical_not(active))
            def _():
                skip(tile)

            return carry

        lax.fori_loop(first, last, step, 0)


def attend_kernel(
    info,
    x0, x1, x2, x3,
    kv0, kv1, kv2, kv3,
    p0, p1, p2, p3,
    d0, d1, d2, d3,
    r0, r1, r2, r3,
    qs, gs, ks, vs, kt, vt, kp, vp, kpt, vpt, dk, dv, dkp, dvp, os, dq, sent, sems,
):
    y = info[0]
    z = info[1]
    length = info[2]
    for s, x in enumerate((x0, x1, x2, x3)):
        block = lax.rem(y - s + NY, NY)
        start = (block * NZ + z) * BLOCK
        valid = (lax.broadcasted_iota(jnp.int32, (BLOCK, HD), 0) + start) < length
        for j in range(HEADS):
            at = aligned((block * HEADS + j) * BLOCK, BLOCK)
            cols = slice(j * HD, (j + 1) * HD)
            qs[at, :] = x[0, :, cols]
            gs[at, :] = jnp.where(valid, x[1, :, cols].astype(F32), 0.0).astype(BF16)
    for s, kv in enumerate((kv0, kv1, kv2, kv3)):
        zp = lax.rem(z - s + NZ, NZ)
        for b in range(NY):
            at = aligned((zp * NY + b) * PROMPT_ROWS, PROMPT_ROWS)
            kp[at, :] = kv[b, 0, :PROMPT_ROWS, :]
            vp[at, :] = kv[b, 1, :PROMPT_ROWS, :]
            at = aligned((b * NZ + zp) * BLOCK, BLOCK)
            k = kv[b, 0, PROMPT_ROWS:, :]
            v = kv[b, 1, PROMPT_ROWS:, :]
            ks[at, :] = k
            vs[at, :] = v
            kt[:, at] = k.T
            vt[:, at] = v.T
    for c in range(PROMPT // BLOCK):
        rows = slice(c * BLOCK, (c + 1) * BLOCK)
        kpt[:, rows] = kp[rows, :].T
        vpt[:, rows] = vp[rows, :].T
    for grad in (dk, dv, dkp, dvp):
        grad[...] = jnp.zeros_like(grad)

    def tile_step(tile, chunks, first_masked):
        at = aligned(tile * TILE, TILE)
        query_pos = tile_positions(tile, z)
        q = qs[at, :]
        qt = q.T
        n = chunks * CHUNK
        first = jnp.dot(kp[...], qt, preferred_element_type=F32)
        s = jnp.dot(ks[:n, :], qt, preferred_element_type=F32)
        s = causal(s, chunks, first_masked, query_pos)
        top = jnp.maximum(
            jnp.max(first, axis=0, keepdims=True), jnp.max(s, axis=0, keepdims=True)
        )
        first = jnp.exp2((first - top) * SCALE2)
        total = jnp.sum(first, axis=0, keepdims=True)
        first = first.astype(BF16)
        out_t = jnp.dot(vpt[...], first, preferred_element_type=F32)
        p = jnp.exp2((s - top) * SCALE2)
        total = total + jnp.sum(p, axis=0, keepdims=True)
        p = p.astype(BF16)
        out_t = out_t + jnp.dot(vt[:, :n], p, preferred_element_type=F32)
        inv = 1.0 / total
        out_t = out_t * inv
        os[at, :] = jnp.where(query_pos < length, out_t, 0.0).T.astype(BF16)
        grad_t = gs[at, :].astype(F32).T
        delta = jnp.sum(grad_t * out_t, axis=0, keepdims=True) * inv
        grad_t = grad_t * inv
        grad = grad_t.T.astype(BF16)
        grad_t = grad_t.astype(BF16)
        dp = jnp.dot(vp[...], grad_t, preferred_element_type=F32)
        ds = (first.astype(F32) * (dp - delta)).astype(BF16)
        dvp[...] += jnp.dot(first, grad, preferred_element_type=F32)
        dkp[...] += jnp.dot(ds, q, preferred_element_type=F32)
        dq_t = jnp.dot(kpt[...], ds, preferred_element_type=F32)
        dp = jnp.dot(vs[:n, :], grad_t, preferred_element_type=F32)
        ds = (p.astype(F32) * (dp - delta)).astype(BF16)
        dv[:n, :] += jnp.dot(p, grad, preferred_element_type=F32)
        dk[:n, :] += jnp.dot(ds, q, preferred_element_type=F32)
        dq_t = dq_t + jnp.dot(kt[:, :n], ds, preferred_element_type=F32)
        dq[at, :] = (dq_t * SCALE).T.astype(BF16)

    def skip(tile):
        at = aligned(tile * TILE, TILE)
        os[at, :] = jnp.zeros((TILE, HD), BF16)
        dq[at, :] = jnp.zeros((TILE, HD), BF16)

    over_tiles(z, length, tile_step, skip)
    copies = []
    for s, r in enumerate((r0, r1, r2, r3)):
        zp = lax.rem(z + s, NZ)
        for b in range(NY):
            at = aligned((b * NZ + zp) * BLOCK, BLOCK)
            sent[s, b, 0] = (dk[at, :] * SCALE).astype(BF16)
            sent[s, b, 1] = dv[at, :].astype(BF16)
        copies.append(pltpu.make_async_copy(sent.at[s], r, sems.at[s]))
        copies[-1].start()
    for s, d in enumerate((d0, d1, d2, d3)):
        d[:GROUP, :] = os[head_rows(y + s), :]
        d[GROUP:, :] = dq[head_rows(y + s), :]
    for s, p in enumerate((p0, p1, p2, p3)):
        zp = lax.rem(z + s, NZ)
        for b in range(NY):
            at = aligned((zp * NY + b) * PROMPT_ROWS, PROMPT_ROWS)
            p[b, 0] = (dkp[at, :] * SCALE).astype(BF16)
            p[b, 1] = dvp[at, :].astype(BF16)
    for copy in copies:
        copy.wait()


def attend(info, rows, keyvals):
    return pl.pallas_call(
        attend_kernel,
        out_shape=[shaped((NY, 2, PROMPT_ROWS, HD), BF16)] * NZ
        + [shaped((2 * GROUP, HD), BF16)] * NY
        + [shaped((NY, 2, BLOCK, HD), BF16)] * NZ,
        in_specs=[SMEM] + [VMEM] * 8,
        out_specs=[VMEM] * 8 + [pl.BlockSpec(memory_space=pl.ANY)] * NZ,
        scratch_shapes=[pltpu.VMEM((ROWS, HD), BF16)] * 2
        + [pltpu.VMEM((RESP, HD), BF16)] * 2
        + [pltpu.VMEM((HD, RESP), BF16)] * 2
        + [pltpu.VMEM((PROMPT, HD), BF16)] * 2
        + [pltpu.VMEM((HD, PROMPT), BF16)] * 2
        + [pltpu.VMEM((RESP, HD), F32)] * 2
        + [pltpu.VMEM((PROMPT, HD), F32)] * 2
        + [pltpu.VMEM((ROWS, HD), BF16)] * 2
        + [pltpu.VMEM((NZ, NY, 2, BLOCK, HD), BF16), pltpu.SemaphoreType.DMA((NZ,))],
        compiler_params=pltpu.CompilerParams(vmem_limit_bytes=48 * 2**20),
        name="attend",
    )(info, *rows, *keyvals)


def settle_kernel(
    info, r0, r1, r2, r3, prompt, p0, p1, p2, p3
):
    y = info[0]
    for s, p in enumerate((p0, p1, p2, p3)):
        b = lax.rem(y + s, NY)
        for i in range(2):
            p[i * PIECE : i * PIECE + PROMPT_ROWS, :] = prompt[b, i].astype(BF16)
            p[i * PIECE + PROMPT_ROWS : (i + 1) * PIECE, :] = (
                (r0[b, i].astype(F32) + r1[b, i].astype(F32))
                + (r2[b, i].astype(F32) + r3[b, i].astype(F32))
            ).astype(BF16)


def settle(info, terms, prompt):
    return pl.pallas_call(
        settle_kernel,
        out_shape=[shaped((2 * PIECE, HD), BF16)] * NY,
        in_specs=[SMEM] + [VMEM] * 5,
        out_specs=[VMEM] * 4,
        compiler_params=pltpu.CompilerParams(vmem_limit_bytes=16 * 2**20),
        name="settle",
    )(info, *terms, prompt)


def rows_kernel(info, d0, d1, d2, d3, att, dq):
    y = info[0]
    for s, d in enumerate((d0, d1, d2, d3)):
        block = lax.rem(y - s + NY, NY)
        for j in range(HEADS):
            at = aligned((block * HEADS + j) * HD, HD)
            att[:, at] = d[j * BLOCK : (j + 1) * BLOCK, :]
            dq[:, at] = d[GROUP + j * BLOCK : GROUP + (j + 1) * BLOCK, :]


def lay_rows(info, pieces):
    return pl.pallas_call(
        rows_kernel,
        out_shape=[shaped((BLOCK, NY * HEADS * HD), BF16)] * 2,
        in_specs=[SMEM] + [VMEM] * 4,
        out_specs=[VMEM] * 2,
        compiler_params=pltpu.CompilerParams(vmem_limit_bytes=16 * 2**20),
        name="lay_rows",
    )(info, *pieces)


def place_kernel(info, done, p0, p1, p2, p3, dk, dv, pk, pv):
    y = info[0]
    for s, p in enumerate((p0, p1, p2, p3)):
        at = aligned(lax.rem(y - s + NY, NY) * HD, HD)
        pk[:, at] = p[:PROMPT_ROWS, :].astype(F32)
        dk[:, at] = p[PROMPT_ROWS:PIECE, :].astype(F32)
        pv[:, at] = p[PIECE : PIECE + PROMPT_ROWS, :].astype(F32)
        dv[:, at] = p[PIECE + PROMPT_ROWS : 2 * PIECE, :].astype(F32)


def place(info, done, pieces):
    out = shaped((BLOCK, NY * HD), F32)
    prompt_out = shaped((PROMPT_ROWS, NY * HD), F32)
    return pl.pallas_call(
        place_kernel,
        out_shape=[out, out, prompt_out, prompt_out],
        in_specs=[SMEM, pl.BlockSpec(memory_space=pl.ANY)] + [VMEM] * 4,
        out_specs=[VMEM] * 4,
        compiler_params=pltpu.CompilerParams(vmem_limit_bytes=16 * 2**20),
        name="place",
    )(info, done, *pieces)


def y_shift(a, s):
    pairs = [(i * NZ + k, (i + s) % NY * NZ + k) for i in range(NY) for k in range(NZ)]
    return lax.ppermute(a, "prefix", pairs)


def z_shift(a, s):
    pairs = [(i * NZ + k, i * NZ + (k + s) % NZ) for i in range(NY) for k in range(NZ)]
    return lax.ppermute(a, "prefix", pairs)


def core_swap(a):
    return lax.ppermute(a, "resp", [(i, i ^ 1) for i in range(16)])


def x_swap(a, bit):
    return lax.ppermute(a, "resp", [(i, i ^ (2 * bit)) for i in range(16)])


def far_swap(a):
    return lax.ppermute(a, "resp", [(i, i ^ 8) for i in range(16)])


def over_responses(terms):
    core = lax.axis_index("resp") % 2
    dk, dv = terms[0], terms[1]
    half = jnp.where(core == 0, dk, dv) + core_swap(jnp.where(core == 0, dv, dk))
    for swap in (lambda a: x_swap(a, 1), lambda a: x_swap(a, 2), far_swap):
        low = half.astype(BF16)
        half = low.astype(F32) + swap(low).astype(F32)
    other = core_swap(half.astype(BF16)).astype(F32)
    half = half.astype(BF16).astype(F32)
    return jnp.stack([jnp.where(core == 0, half, other), jnp.where(core == 0, other, half)])


def by_y(pieces):
    return [pieces[0]] + [y_shift(pieces[s], s) for s in range(1, NY)]


def by_z(pieces):
    return [pieces[0]] + [z_shift(pieces[s], s) for s in range(1, NZ)]


def per_device(
    response_queries,
    response_keys,
    response_values,
    prompt_keys,
    prompt_values,
    output_grad,
    lengths,
):
    prefix = lax.axis_index("prefix")
    y, z = prefix // NZ, prefix % NZ
    info = jnp.stack([y, z, lengths[lax.axis_index("resp")]]).astype(jnp.int32)
    pick = lax.dynamic_index_in_dim

    def split(a, width):
        return [
            lax.dynamic_slice_in_dim(a, (y + s) % NY * width, width, a.ndim - 1)
            for s in range(NY)
        ]

    keyvals = jnp.stack(
        [
            jnp.concatenate([prompt_keys, response_keys[0]], axis=0),
            jnp.concatenate([prompt_values, response_values[0]], axis=0),
        ]
    )
    keyvals = by_y(split(keyvals, HD))
    *keyvals, queries, grads = lax.optimization_barrier(
        (*keyvals, response_queries[0], output_grad[0])
    )
    stacked = jnp.stack(keyvals)
    keyvals = jnp.stack([pick(stacked, (y - b) % NY, 0, keepdims=False) for b in range(NY)])
    keyvals = by_z([keyvals] * NZ)
    rows = by_y(split(jnp.stack([queries, grads]), HEADS * HD))

    results = attend(info, rows, keyvals)
    prompt_terms = by_z(results[:4])
    d0, d1, d2, d3 = results[4:8]
    d1, d3 = y_shift(d1, 1), y_shift(d3, 3)
    *prompt_terms, d1, d3, d2, t1, t2, t3 = lax.optimization_barrier(
        (*prompt_terms, d1, d3, d2, *results[9:])
    )
    prompt = sum(t.astype(F32) for t in prompt_terms)
    prompt = prompt.transpose(1, 0, 2, 3).reshape(2, NY * PROMPT_ROWS, HD)
    once = jnp.minimum(lengths[0], 1)
    terms = by_z([results[8], t1, t2, t3])
    d2 = y_shift(d2, 2)
    prompt = lax.fori_loop(0, once, lambda i, terms: over_responses(terms), prompt)
    prompt = prompt.reshape(2, NY, PROMPT_ROWS, HD).transpose(1, 0, 2, 3)
    pieces = settle(info, terms, prompt)
    d2, *pieces = lax.optimization_barrier((d2, *pieces))
    attention_out, query_grad = lay_rows(info, (d0, d1, d2, d3))
    key_own, value_own, prompt_key_grad, prompt_value_grad = place(
        info, query_grad, by_y(pieces)
    )
    return (
        attention_out[None],
        query_grad[None],
        key_own[None],
        value_own[None],
        prompt_key_grad,
        prompt_value_grad,
    )


def solution(mesh):
    return jax.shard_map(
        per_device,
        mesh=mesh,
        in_specs=(
            P("resp", "prefix", None),
            P("resp", "prefix", None),
            P("resp", "prefix", None),
            P("prefix", None),
            P("prefix", None),
            P("resp", "prefix", None),
            P(),
        ),
        out_specs=(
            P("resp", "prefix", None),
            P("resp", "prefix", None),
            P("resp", "prefix", None),
            P("resp", "prefix", None),
            P("prefix", None),
            P("prefix", None),
        ),
        check_vma=False,
    )
```

```python
import math

import jax
import jax.numpy as jnp
from jax import lax
from jax.experimental import pallas as pl
from jax.experimental.pallas import tpu as pltpu
from jax.sharding import PartitionSpec as P

HD = 128
BLOCK = 128
PROMPT_ROWS = 48
PIECE = PROMPT_ROWS + BLOCK
HEADS = 5
NY = 4
NZ = 4
PROMPT = PROMPT_ROWS * NY * NZ
KEYS = PROMPT + BLOCK * NY * NZ
ROWS = NY * HEADS * BLOCK
CHUNK = 256
TILE = 256
MASKED = -1e30
SCALE = 1.0 / math.sqrt(HD)
SCALE2 = SCALE * math.log2(math.e)
F32 = jnp.float32
BF16 = jnp.bfloat16
CLASSES = ((0, 2, 2, 0), (2, 5, 4, 0), (5, 7, 6, 4), (7, 10, 8, 4))
TILES = ROWS // TILE
RESP = KEYS - PROMPT
GROUP = HEADS * BLOCK
VMEM = pl.BlockSpec(memory_space=pltpu.VMEM)
SMEM = pl.BlockSpec(memory_space=pltpu.SMEM)


def shaped(shape, dtype):
    return jax.ShapeDtypeStruct(shape, dtype)


def aligned(start, size):
    return pl.ds(pl.multiple_of(start, size), size)


def head_rows(block):
    return aligned(lax.rem(block, NY) * GROUP, GROUP)


def tile_positions(tile, z):
    u = tile * 2
    lane = lax.broadcasted_iota(jnp.int32, (1, TILE), 1)
    low = (u // HEADS * NZ + z) * BLOCK
    high = ((u + 1) // HEADS * NZ + z) * BLOCK - BLOCK
    return lane + jnp.where(lane < BLOCK, low, high)


def causal(s, chunks, first_masked, query_pos):
    end, start = chunks * CHUNK, first_masked * CHUNK
    key_pos = lax.broadcasted_iota(jnp.int32, (end - start, TILE), 0) + start
    last = jnp.where(key_pos <= query_pos, s[start:], MASKED)
    return jnp.concatenate([s[:start], last]) if start else last


def over_tiles(z, length, body, skip):
    for first, last, chunks, first_masked in CLASSES:

        def step(tile, carry, chunks=chunks, first_masked=first_masked):
            active = (tile * 2 // HEADS * NZ + z) * BLOCK < length

            @pl.when(active)
            def _():
                body(tile, chunks, first_masked)

            @pl.when(jnp.logical_not(active))
            def _():
                skip(tile)

            return carry

        lax.fori_loop(first, last, step, 0)


def attend_kernel(
    info,
    x0, x1, x2, x3,
    kv0, kv1, kv2, kv3,
    p0, p1, p2, p3,
    d0, d1, d2, d3,
    r0, r1, r2, r3,
    qs, gs, ks, vs, kt, vt, kp, vp, kpt, vpt, dk, dv, dkp, dvp, os, dq, sent, moved, sems,
):
    y = info[0]
    z = info[1]
    length = info[2]
    for s, x in enumerate((x0, x1, x2, x3)):
        block = lax.rem(y - s + NY, NY)
        start = (block * NZ + z) * BLOCK
        valid = (lax.broadcasted_iota(jnp.int32, (BLOCK, HD), 0) + start) < length
        for j in range(HEADS):
            at = aligned((block * HEADS + j) * BLOCK, BLOCK)
            cols = slice(j * HD, (j + 1) * HD)
            qs[at, :] = x[0, :, cols]
            gs[at, :] = jnp.where(valid, x[1, :, cols].astype(F32), 0.0).astype(BF16)
    for s, kv in enumerate((kv0, kv1, kv2, kv3)):
        zp = lax.rem(z - s + NZ, NZ)
        for b in range(NY):
            at = aligned((zp * NY + b) * PROMPT_ROWS, PROMPT_ROWS)
            kp[at, :] = kv[b, 0, :PROMPT_ROWS, :]
            vp[at, :] = kv[b, 1, :PROMPT_ROWS, :]
            at = aligned((b * NZ + zp) * BLOCK, BLOCK)
            k = kv[b, 0, PROMPT_ROWS:, :]
            v = kv[b, 1, PROMPT_ROWS:, :]
            ks[at, :] = k
            vs[at, :] = v
            kt[:, at] = k.T
            vt[:, at] = v.T
    for c in range(PROMPT // BLOCK):
        rows = slice(c * BLOCK, (c + 1) * BLOCK)
        kpt[:, rows] = kp[rows, :].T
        vpt[:, rows] = vp[rows, :].T
    for grad in (dk, dv, dkp, dvp):
        grad[...] = jnp.zeros_like(grad)

    def tile_step(tile, chunks, first_masked):
        at = aligned(tile * TILE, TILE)
        query_pos = tile_positions(tile, z)
        q = qs[at, :]
        qt = q.T
        n = chunks * CHUNK
        first = jnp.dot(kp[...], qt, preferred_element_type=F32)
        s = jnp.dot(ks[:n, :], qt, preferred_element_type=F32)
        s = causal(s, chunks, first_masked, query_pos)
        top = jnp.maximum(
            jnp.max(first, axis=0, keepdims=True), jnp.max(s, axis=0, keepdims=True)
        )
        first = jnp.exp2((first - top) * SCALE2)
        total = jnp.sum(first, axis=0, keepdims=True)
        first = first.astype(BF16)
        out_t = jnp.dot(vpt[...], first, preferred_element_type=F32)
        p = jnp.exp2((s - top) * SCALE2)
        total = total + jnp.sum(p, axis=0, keepdims=True)
        p = p.astype(BF16)
        out_t = out_t + jnp.dot(vt[:, :n], p, preferred_element_type=F32)
        inv = 1.0 / total
        out_t = out_t * inv
        os[at, :] = jnp.where(query_pos < length, out_t, 0.0).T.astype(BF16)
        grad_t = gs[at, :].astype(F32).T
        delta = jnp.sum(grad_t * out_t, axis=0, keepdims=True) * inv
        grad_t = grad_t * inv
        grad = grad_t.T.astype(BF16)
        grad_t = grad_t.astype(BF16)
        dp = jnp.dot(vp[...], grad_t, preferred_element_type=F32)
        ds = (first.astype(F32) * (dp - delta)).astype(BF16)
        dvp[...] += jnp.dot(first, grad, preferred_element_type=F32)
        dkp[...] += jnp.dot(ds, q, preferred_element_type=F32)
        dq_t = jnp.dot(kpt[...], ds, preferred_element_type=F32)
        dp = jnp.dot(vs[:n, :], grad_t, preferred_element_type=F32)
        ds = (p.astype(F32) * (dp - delta)).astype(BF16)
        dv[:n, :] += jnp.dot(p, grad, preferred_element_type=F32)
        dk[:n, :] += jnp.dot(ds, q, preferred_element_type=F32)
        dq_t = dq_t + jnp.dot(kt[:, :n], ds, preferred_element_type=F32)
        dq[at, :] = (dq_t * SCALE).T.astype(BF16)

    def skip(tile):
        at = aligned(tile * TILE, TILE)
        os[at, :] = jnp.zeros((TILE, HD), BF16)
        dq[at, :] = jnp.zeros((TILE, HD), BF16)

    over_tiles(z, length, tile_step, skip)
    copies = []
    for s, r in enumerate((r0, r1, r2, r3)):
        zp = lax.rem(z + s, NZ)
        for b in range(NY):
            at = aligned((b * NZ + zp) * BLOCK, BLOCK)
            sent[s, b, 0] = (dk[at, :] * SCALE).astype(BF16)
            sent[s, b, 1] = dv[at, :].astype(BF16)
        copies.append(pltpu.make_async_copy(sent.at[s], r, sems.at[s]))
        copies[-1].start()
    for s, d in enumerate((d0, d1, d2, d3)):
        moved[s, :GROUP, :] = os[head_rows(y + s), :]
        moved[s, GROUP:, :] = dq[head_rows(y + s), :]
        copies.append(pltpu.make_async_copy(moved.at[s], d, sems.at[NZ + s]))
        copies[-1].start()
    for s, p in enumerate((p0, p1, p2, p3)):
        zp = lax.rem(z + s, NZ)
        for b in range(NY):
            at = aligned((zp * NY + b) * PROMPT_ROWS, PROMPT_ROWS)
            p[b, 0] = (dkp[at, :] * SCALE).astype(BF16)
            p[b, 1] = dvp[at, :].astype(BF16)
    for copy in copies:
        copy.wait()


def attend(info, rows, keyvals):
    return pl.pallas_call(
        attend_kernel,
        out_shape=[shaped((NY, 2, PROMPT_ROWS, HD), BF16)] * NZ
        + [shaped((2 * GROUP, HD), BF16)] * NY
        + [shaped((NY, 2, BLOCK, HD), BF16)] * NZ,
        in_specs=[SMEM] + [VMEM] * 8,
        out_specs=[VMEM] * NZ + [pl.BlockSpec(memory_space=pl.ANY)] * (NY + NZ),
        scratch_shapes=[pltpu.VMEM((ROWS, HD), BF16)] * 2
        + [pltpu.VMEM((RESP, HD), BF16)] * 2
        + [pltpu.VMEM((HD, RESP), BF16)] * 2
        + [pltpu.VMEM((PROMPT, HD), BF16)] * 2
        + [pltpu.VMEM((HD, PROMPT), BF16)] * 2
        + [pltpu.VMEM((RESP, HD), F32)] * 2
        + [pltpu.VMEM((PROMPT, HD), F32)] * 2
        + [pltpu.VMEM((ROWS, HD), BF16)] * 2
        + [
            pltpu.VMEM((NZ, NY, 2, BLOCK, HD), BF16),
            pltpu.VMEM((NY, 2 * GROUP, HD), BF16),
            pltpu.SemaphoreType.DMA((NZ + NY,)),
        ],
        compiler_params=pltpu.CompilerParams(vmem_limit_bytes=48 * 2**20),
        name="attend",
    )(info, *rows, *keyvals)


def settle_kernel(
    info, r0, r1, r2, r3, prompt, p0, p1, p2, p3
):
    y = info[0]
    for s, p in enumerate((p0, p1, p2, p3)):
        b = lax.rem(y + s, NY)
        for i in range(2):
            p[i * PIECE : i * PIECE + PROMPT_ROWS, :] = prompt[b, i].astype(BF16)
            p[i * PIECE + PROMPT_ROWS : (i + 1) * PIECE, :] = (
                (r0[b, i].astype(F32) + r1[b, i].astype(F32))
                + (r2[b, i].astype(F32) + r3[b, i].astype(F32))
            ).astype(BF16)


def settle(info, terms, prompt):
    return pl.pallas_call(
        settle_kernel,
        out_shape=[shaped((2 * PIECE, HD), BF16)] * NY,
        in_specs=[SMEM] + [VMEM] * 5,
        out_specs=[VMEM] * 4,
        compiler_params=pltpu.CompilerParams(vmem_limit_bytes=16 * 2**20),
        name="settle",
    )(info, *terms, prompt)


def rows_kernel(info, d0, d1, d2, d3, att, dq, done):
    y = info[0]
    done[...] = jnp.zeros_like(done)
    for s, d in enumerate((d0, d1, d2, d3)):
        block = lax.rem(y - s + NY, NY)
        for j in range(HEADS):
            at = aligned((block * HEADS + j) * HD, HD)
            att[:, at] = d[j * BLOCK : (j + 1) * BLOCK, :]
            dq[:, at] = d[GROUP + j * BLOCK : GROUP + (j + 1) * BLOCK, :]


def lay_rows(info, pieces):
    return pl.pallas_call(
        rows_kernel,
        out_shape=[shaped((BLOCK, NY * HEADS * HD), BF16)] * 2 + [shaped((8, HD), F32)],
        in_specs=[SMEM] + [VMEM] * 4,
        out_specs=[VMEM] * 3,
        compiler_params=pltpu.CompilerParams(vmem_limit_bytes=16 * 2**20),
        name="lay_rows",
    )(info, *pieces)


def place_kernel(info, done, p0, p1, p2, p3, dk, dv, pk, pv):
    y = info[0]
    for s, p in enumerate((p0, p1, p2, p3)):
        at = aligned(lax.rem(y - s + NY, NY) * HD, HD)
        pk[:, at] = p[:PROMPT_ROWS, :].astype(F32)
        dk[:, at] = p[PROMPT_ROWS:PIECE, :].astype(F32)
        pv[:, at] = p[PIECE : PIECE + PROMPT_ROWS, :].astype(F32)
        dv[:, at] = p[PIECE + PROMPT_ROWS : 2 * PIECE, :].astype(F32)


def place(info, done, pieces):
    out = shaped((BLOCK, NY * HD), F32)
    prompt_out = shaped((PROMPT_ROWS, NY * HD), F32)
    return pl.pallas_call(
        place_kernel,
        out_shape=[out, out, prompt_out, prompt_out],
        in_specs=[SMEM, pl.BlockSpec(memory_space=pl.ANY)] + [VMEM] * 4,
        out_specs=[VMEM] * 4,
        compiler_params=pltpu.CompilerParams(vmem_limit_bytes=16 * 2**20),
        name="place",
    )(info, done, *pieces)


def y_shift(a, s):
    pairs = [(i * NZ + k, (i + s) % NY * NZ + k) for i in range(NY) for k in range(NZ)]
    return lax.ppermute(a, "prefix", pairs)


def z_shift(a, s):
    pairs = [(i * NZ + k, i * NZ + (k + s) % NZ) for i in range(NY) for k in range(NZ)]
    return lax.ppermute(a, "prefix", pairs)


def core_swap(a):
    return lax.ppermute(a, "resp", [(i, i ^ 1) for i in range(16)])


def x_swap(a, bit):
    return lax.ppermute(a, "resp", [(i, i ^ (2 * bit)) for i in range(16)])


def far_swap(a):
    return lax.ppermute(a, "resp", [(i, i ^ 8) for i in range(16)])


def over_responses(terms):
    core = lax.axis_index("resp") % 2
    dk, dv = terms[0], terms[1]
    half = jnp.where(core == 0, dk, dv) + core_swap(jnp.where(core == 0, dv, dk))
    for swap in (lambda a: x_swap(a, 1), lambda a: x_swap(a, 2), far_swap):
        low = half.astype(BF16)
        half = low.astype(F32) + swap(low).astype(F32)
    other = core_swap(half.astype(BF16)).astype(F32)
    half = half.astype(BF16).astype(F32)
    return jnp.stack([jnp.where(core == 0, half, other), jnp.where(core == 0, other, half)])


def by_y(pieces):
    return [pieces[0]] + [y_shift(pieces[s], s) for s in range(1, NY)]


def by_z(pieces):
    return [pieces[0]] + [z_shift(pieces[s], s) for s in range(1, NZ)]


def per_device(
    response_queries,
    response_keys,
    response_values,
    prompt_keys,
    prompt_values,
    output_grad,
    lengths,
):
    prefix = lax.axis_index("prefix")
    y, z = prefix // NZ, prefix % NZ
    info = jnp.stack([y, z, lengths[lax.axis_index("resp")]]).astype(jnp.int32)
    pick = lax.dynamic_index_in_dim

    def split(a, width):
        return [
            lax.dynamic_slice_in_dim(a, (y + s) % NY * width, width, a.ndim - 1)
            for s in range(NY)
        ]

    keyvals = jnp.stack(
        [
            jnp.concatenate([prompt_keys, response_keys[0]], axis=0),
            jnp.concatenate([prompt_values, response_values[0]], axis=0),
        ]
    )
    keyvals = by_y(split(keyvals, HD))
    *keyvals, queries, grads = lax.optimization_barrier(
        (*keyvals, response_queries[0], output_grad[0])
    )
    stacked = jnp.stack(keyvals)
    keyvals = jnp.stack([pick(stacked, (y - b) % NY, 0, keepdims=False) for b in range(NY)])
    keyvals = by_z([keyvals] * NZ)
    rows = by_y(split(jnp.stack([queries, grads]), HEADS * HD))

    results = attend(info, rows, keyvals)
    prompt_terms = by_z(results[:4])
    d0, d1, d2, d3 = results[4:8]
    prompt_terms[1], d1, d3 = lax.optimization_barrier((prompt_terms[1], d1, d3))
    d1, d3 = y_shift(d1, 1), y_shift(d3, 3)
    *prompt_terms, t1, t2, t3 = lax.optimization_barrier((*prompt_terms, *results[9:]))
    prompt = sum(t.astype(F32) for t in prompt_terms)
    prompt = prompt.transpose(1, 0, 2, 3).reshape(2, NY * PROMPT_ROWS, HD)
    once = jnp.minimum(lengths[0], 1)
    terms = by_z([results[8], t1, t2, t3])
    prompt, d1, d3, d2 = lax.optimization_barrier((prompt, d1, d3, d2))
    d2 = y_shift(d2, 2)
    prompt = lax.fori_loop(0, once, lambda i, terms: over_responses(terms), prompt)
    prompt = prompt.reshape(2, NY, PROMPT_ROWS, HD).transpose(1, 0, 2, 3)
    pieces = settle(info, terms, prompt)
    d2, *pieces = lax.optimization_barrier((d2, *pieces))
    attention_out, query_grad, done = lay_rows(info, (d0, d1, d2, d3))
    key_own, value_own, prompt_key_grad, prompt_value_grad = place(
        info, done, by_y(pieces)
    )
    return (
        attention_out[None],
        query_grad[None],
        key_own[None],
        value_own[None],
        prompt_key_grad,
        prompt_value_grad,
    )


def solution(mesh):
    return jax.shard_map(
        per_device,
        mesh=mesh,
        in_specs=(
            P("resp", "prefix", None),
            P("resp", "prefix", None),
            P("resp", "prefix", None),
            P("prefix", None),
            P("prefix", None),
            P("resp", "prefix", None),
            P(),
        ),
        out_specs=(
            P("resp", "prefix", None),
            P("resp", "prefix", None),
            P("resp", "prefix", None),
            P("resp", "prefix", None),
            P("prefix", None),
            P("prefix", None),
        ),
        check_vma=False,
    )
```

```python
import math

import jax
import jax.numpy as jnp
from jax import lax
from jax.experimental import pallas as pl
from jax.experimental.pallas import tpu as pltpu
from jax.sharding import PartitionSpec as P

HD = 128
BLOCK = 128
PROMPT_ROWS = 48
PIECE = PROMPT_ROWS + BLOCK
HEADS = 5
NY = 4
NZ = 4
PROMPT = PROMPT_ROWS * NY * NZ
KEYS = PROMPT + BLOCK * NY * NZ
ROWS = NY * HEADS * BLOCK
CHUNK = 256
TILE = 256
MASKED = -1e30
SCALE = 1.0 / math.sqrt(HD)
SCALE2 = SCALE * math.log2(math.e)
F32 = jnp.float32
BF16 = jnp.bfloat16
CLASSES = ((0, 2, 2, 0), (2, 5, 4, 0), (5, 7, 6, 4), (7, 10, 8, 4))
TILES = ROWS // TILE
RESP = KEYS - PROMPT
GROUP = HEADS * BLOCK
VMEM = pl.BlockSpec(memory_space=pltpu.VMEM)
SMEM = pl.BlockSpec(memory_space=pltpu.SMEM)


def shaped(shape, dtype):
    return jax.ShapeDtypeStruct(shape, dtype)


def aligned(start, size):
    return pl.ds(pl.multiple_of(start, size), size)


def head_rows(block):
    return aligned(lax.rem(block, NY) * GROUP, GROUP)


def tile_positions(tile, z):
    u = tile * 2
    lane = lax.broadcasted_iota(jnp.int32, (1, TILE), 1)
    low = (u // HEADS * NZ + z) * BLOCK
    high = ((u + 1) // HEADS * NZ + z) * BLOCK - BLOCK
    return lane + jnp.where(lane < BLOCK, low, high)


def causal(s, chunks, first_masked, query_pos):
    end, start = chunks * CHUNK, first_masked * CHUNK
    key_pos = lax.broadcasted_iota(jnp.int32, (end - start, TILE), 0) + start
    last = jnp.where(key_pos <= query_pos, s[start:], MASKED)
    return jnp.concatenate([s[:start], last]) if start else last


def over_tiles(z, length, body, skip):
    for first, last, chunks, first_masked in CLASSES:

        def step(tile, carry, chunks=chunks, first_masked=first_masked):
            active = (tile * 2 // HEADS * NZ + z) * BLOCK < length

            @pl.when(active)
            def _():
                body(tile, chunks, first_masked)

            @pl.when(jnp.logical_not(active))
            def _():
                skip(tile)

            return carry

        lax.fori_loop(first, last, step, 0)


def attend_kernel(
    info,
    x0, x1, x2, x3,
    kv0, kv1, kv2, kv3,
    p0, p1, p2, p3,
    d0, d1, d2, d3,
    r0, r1, r2, r3,
    qs, gs, ks, vs, kt, vt, kp, vp, kpt, vpt, dk, dv, dkp, dvp, os, dq, sent, moved, sems,
):
    y = info[0]
    z = info[1]
    length = info[2]
    for s, x in enumerate((x0, x1, x2, x3)):
        block = lax.rem(y - s + NY, NY)
        start = (block * NZ + z) * BLOCK
        valid = (lax.broadcasted_iota(jnp.int32, (BLOCK, HD), 0) + start) < length
        for j in range(HEADS):
            at = aligned((block * HEADS + j) * BLOCK, BLOCK)
            cols = slice(j * HD, (j + 1) * HD)
            qs[at, :] = x[0, :, cols]
            gs[at, :] = jnp.where(valid, x[1, :, cols].astype(F32), 0.0).astype(BF16)
    for s, kv in enumerate((kv0, kv1, kv2, kv3)):
        zp = lax.rem(z - s + NZ, NZ)
        for b in range(NY):
            at = aligned((zp * NY + b) * PROMPT_ROWS, PROMPT_ROWS)
            kp[at, :] = kv[b, 0, :PROMPT_ROWS, :]
            vp[at, :] = kv[b, 1, :PROMPT_ROWS, :]
            at = aligned((b * NZ + zp) * BLOCK, BLOCK)
            k = kv[b, 0, PROMPT_ROWS:, :]
            v = kv[b, 1, PROMPT_ROWS:, :]
            ks[at, :] = k
            vs[at, :] = v
            kt[:, at] = k.T
            vt[:, at] = v.T
    for c in range(PROMPT // BLOCK):
        rows = slice(c * BLOCK, (c + 1) * BLOCK)
        kpt[:, rows] = kp[rows, :].T
        vpt[:, rows] = vp[rows, :].T
    for grad in (dk, dv, dkp, dvp):
        grad[...] = jnp.zeros_like(grad)

    def tile_step(tile, chunks, first_masked):
        at = aligned(tile * TILE, TILE)
        query_pos = tile_positions(tile, z)
        q = qs[at, :]
        qt = q.T
        n = chunks * CHUNK
        first = jnp.dot(kp[...], qt, preferred_element_type=F32)
        s = jnp.dot(ks[:n, :], qt, preferred_element_type=F32)
        s = causal(s, chunks, first_masked, query_pos)
        top = jnp.maximum(
            jnp.max(first, axis=0, keepdims=True), jnp.max(s, axis=0, keepdims=True)
        )
        first = jnp.exp2((first - top) * SCALE2)
        total = jnp.sum(first, axis=0, keepdims=True)
        first = first.astype(BF16)
        out_t = jnp.dot(vpt[...], first, preferred_element_type=F32)
        p = jnp.exp2((s - top) * SCALE2)
        total = total + jnp.sum(p, axis=0, keepdims=True)
        p = p.astype(BF16)
        out_t = out_t + jnp.dot(vt[:, :n], p, preferred_element_type=F32)
        inv = 1.0 / total
        out_t = out_t * inv
        os[at, :] = jnp.where(query_pos < length, out_t, 0.0).T.astype(BF16)
        grad_t = gs[at, :].astype(F32).T
        delta = jnp.sum(grad_t * out_t, axis=0, keepdims=True) * inv
        grad_t = grad_t * inv
        grad = grad_t.T.astype(BF16)
        grad_t = grad_t.astype(BF16)
        dp = jnp.dot(vp[...], grad_t, preferred_element_type=F32)
        ds = (first.astype(F32) * (dp - delta)).astype(BF16)
        dvp[...] += jnp.dot(first, grad, preferred_element_type=F32)
        dkp[...] += jnp.dot(ds, q, preferred_element_type=F32)
        dq_t = jnp.dot(kpt[...], ds, preferred_element_type=F32)
        dp = jnp.dot(vs[:n, :], grad_t, preferred_element_type=F32)
        ds = (p.astype(F32) * (dp - delta)).astype(BF16)
        dv[:n, :] += jnp.dot(p, grad, preferred_element_type=F32)
        dk[:n, :] += jnp.dot(ds, q, preferred_element_type=F32)
        dq_t = dq_t + jnp.dot(kt[:, :n], ds, preferred_element_type=F32)
        dq[at, :] = (dq_t * SCALE).T.astype(BF16)

    def skip(tile):
        at = aligned(tile * TILE, TILE)
        os[at, :] = jnp.zeros((TILE, HD), BF16)
        dq[at, :] = jnp.zeros((TILE, HD), BF16)

    over_tiles(z, length, tile_step, skip)
    copies = []
    for s, r in enumerate((r0, r1, r2, r3)):
        zp = lax.rem(z + s, NZ)
        for b in range(NY):
            at = aligned((b * NZ + zp) * BLOCK, BLOCK)
            sent[s, b, 0] = (dk[at, :] * SCALE).astype(BF16)
            sent[s, b, 1] = dv[at, :].astype(BF16)
        copies.append(pltpu.make_async_copy(sent.at[s], r, sems.at[s]))
        copies[-1].start()
    for s, d in enumerate((d0, d1, d2, d3)):
        moved[s, :GROUP, :] = os[head_rows(y + s), :]
        moved[s, GROUP:, :] = dq[head_rows(y + s), :]
        copies.append(pltpu.make_async_copy(moved.at[s], d, sems.at[NZ + s]))
        copies[-1].start()
    for s, p in enumerate((p0, p1, p2, p3)):
        zp = lax.rem(z + s, NZ)
        for b in range(NY):
            at = aligned((zp * NY + b) * PROMPT_ROWS, PROMPT_ROWS)
            p[b, 0] = (dkp[at, :] * SCALE).astype(BF16)
            p[b, 1] = dvp[at, :].astype(BF16)
    for copy in copies:
        copy.wait()


def attend(info, rows, keyvals):
    return pl.pallas_call(
        attend_kernel,
        out_shape=[shaped((NY, 2, PROMPT_ROWS, HD), BF16)] * NZ
        + [pltpu.HBM((2 * GROUP, HD), BF16)] * NY
        + [pltpu.HBM((NY, 2, BLOCK, HD), BF16)] * NZ,
        in_specs=[SMEM] + [VMEM] * 8,
        out_specs=[VMEM] * NZ + [pl.BlockSpec(memory_space=pltpu.HBM)] * (NY + NZ),
        scratch_shapes=[pltpu.VMEM((ROWS, HD), BF16)] * 2
        + [pltpu.VMEM((RESP, HD), BF16)] * 2
        + [pltpu.VMEM((HD, RESP), BF16)] * 2
        + [pltpu.VMEM((PROMPT, HD), BF16)] * 2
        + [pltpu.VMEM((HD, PROMPT), BF16)] * 2
        + [pltpu.VMEM((RESP, HD), F32)] * 2
        + [pltpu.VMEM((PROMPT, HD), F32)] * 2
        + [pltpu.VMEM((ROWS, HD), BF16)] * 2
        + [
            pltpu.VMEM((NZ, NY, 2, BLOCK, HD), BF16),
            pltpu.VMEM((NY, 2 * GROUP, HD), BF16),
            pltpu.SemaphoreType.DMA((NZ + NY,)),
        ],
        compiler_params=pltpu.CompilerParams(vmem_limit_bytes=48 * 2**20),
        name="attend",
    )(info, *rows, *keyvals)


def settle_kernel(
    info, r0, r1, r2, r3, prompt, p0, p1, p2, p3
):
    y = info[0]
    for s, p in enumerate((p0, p1, p2, p3)):
        b = lax.rem(y + s, NY)
        for i in range(2):
            p[i * PIECE : i * PIECE + PROMPT_ROWS, :] = prompt[b, i].astype(BF16)
            p[i * PIECE + PROMPT_ROWS : (i + 1) * PIECE, :] = (
                (r0[b, i].astype(F32) + r1[b, i].astype(F32))
                + (r2[b, i].astype(F32) + r3[b, i].astype(F32))
            ).astype(BF16)


def settle(info, terms, prompt):
    return pl.pallas_call(
        settle_kernel,
        out_shape=[shaped((2 * PIECE, HD), BF16)] * NY,
        in_specs=[SMEM] + [VMEM] * 5,
        out_specs=[VMEM] * 4,
        compiler_params=pltpu.CompilerParams(vmem_limit_bytes=16 * 2**20),
        name="settle",
    )(info, *terms, prompt)


def rows_kernel(info, d0, d1, d2, d3, att, dq, done):
    y = info[0]
    done[...] = jnp.zeros_like(done)
    for s, d in enumerate((d0, d1, d2, d3)):
        block = lax.rem(y - s + NY, NY)
        for j in range(HEADS):
            at = aligned((block * HEADS + j) * HD, HD)
            att[:, at] = d[j * BLOCK : (j + 1) * BLOCK, :]
            dq[:, at] = d[GROUP + j * BLOCK : GROUP + (j + 1) * BLOCK, :]


def lay_rows(info, pieces):
    return pl.pallas_call(
        rows_kernel,
        out_shape=[shaped((BLOCK, NY * HEADS * HD), BF16)] * 2 + [shaped((8, HD), F32)],
        in_specs=[SMEM] + [VMEM] * 4,
        out_specs=[VMEM] * 3,
        compiler_params=pltpu.CompilerParams(vmem_limit_bytes=16 * 2**20),
        name="lay_rows",
    )(info, *pieces)


def place_kernel(info, done, p0, p1, p2, p3, dk, dv, pk, pv):
    y = info[0]
    for s, p in enumerate((p0, p1, p2, p3)):
        at = aligned(lax.rem(y - s + NY, NY) * HD, HD)
        pk[:, at] = p[:PROMPT_ROWS, :].astype(F32)
        dk[:, at] = p[PROMPT_ROWS:PIECE, :].astype(F32)
        pv[:, at] = p[PIECE : PIECE + PROMPT_ROWS, :].astype(F32)
        dv[:, at] = p[PIECE + PROMPT_ROWS : 2 * PIECE, :].astype(F32)


def place(info, done, pieces):
    out = shaped((BLOCK, NY * HD), F32)
    prompt_out = shaped((PROMPT_ROWS, NY * HD), F32)
    return pl.pallas_call(
        place_kernel,
        out_shape=[out, out, prompt_out, prompt_out],
        in_specs=[SMEM, pl.BlockSpec(memory_space=pl.ANY)] + [VMEM] * 4,
        out_specs=[VMEM] * 4,
        compiler_params=pltpu.CompilerParams(vmem_limit_bytes=16 * 2**20),
        name="place",
    )(info, done, *pieces)


def y_shift(a, s):
    pairs = [(i * NZ + k, (i + s) % NY * NZ + k) for i in range(NY) for k in range(NZ)]
    return lax.ppermute(a, "prefix", pairs)


def z_shift(a, s):
    pairs = [(i * NZ + k, i * NZ + (k + s) % NZ) for i in range(NY) for k in range(NZ)]
    return lax.ppermute(a, "prefix", pairs)


def core_swap(a):
    return lax.ppermute(a, "resp", [(i, i ^ 1) for i in range(16)])


def x_swap(a, bit):
    return lax.ppermute(a, "resp", [(i, i ^ (2 * bit)) for i in range(16)])


def far_swap(a):
    return lax.ppermute(a, "resp", [(i, i ^ 8) for i in range(16)])


def over_responses(terms):
    for swap in (core_swap, lambda a: x_swap(a, 1), lambda a: x_swap(a, 2), far_swap):
        low = terms.astype(BF16)
        terms = low.astype(F32) + swap(low).astype(F32)
    return terms


def by_y(pieces):
    return [pieces[0]] + [y_shift(pieces[s], s) for s in range(1, NY)]


def by_z(pieces):
    return [pieces[0]] + [z_shift(pieces[s], s) for s in range(1, NZ)]


def per_device(
    response_queries,
    response_keys,
    response_values,
    prompt_keys,
    prompt_values,
    output_grad,
    lengths,
):
    prefix = lax.axis_index("prefix")
    y, z = prefix // NZ, prefix % NZ
    info = jnp.stack([y, z, lengths[lax.axis_index("resp")]]).astype(jnp.int32)
    pick = lax.dynamic_index_in_dim

    def split(a, width):
        return [
            lax.dynamic_slice_in_dim(a, (y + s) % NY * width, width, a.ndim - 1)
            for s in range(NY)
        ]

    keyvals = jnp.stack(
        [
            jnp.concatenate([prompt_keys, response_keys[0]], axis=0),
            jnp.concatenate([prompt_values, response_values[0]], axis=0),
        ]
    )
    keyvals = by_y(split(keyvals, HD))
    *keyvals, queries, grads = lax.optimization_barrier(
        (*keyvals, response_queries[0], output_grad[0])
    )
    stacked = jnp.stack(keyvals)
    keyvals = jnp.stack([pick(stacked, (y - b) % NY, 0, keepdims=False) for b in range(NY)])
    keyvals = by_z([keyvals] * NZ)
    rows = by_y(split(jnp.stack([queries, grads]), HEADS * HD))

    results = attend(info, rows, keyvals)
    prompt_terms = by_z(results[:4])
    d0, d1, d2, d3 = results[4:8]
    prompt_terms[1], d1, d3 = lax.optimization_barrier((prompt_terms[1], d1, d3))
    d1, d3 = y_shift(d1, 1), y_shift(d3, 3)
    *prompt_terms, t1, t2, t3 = lax.optimization_barrier((*prompt_terms, *results[9:]))
    prompt = sum(t.astype(F32) for t in prompt_terms)
    prompt = prompt.transpose(1, 0, 2, 3).reshape(2, NY * PROMPT_ROWS, HD)
    once = jnp.minimum(lengths[0], 1)
    terms = by_z([results[8], t1, t2, t3])
    prompt, d1, d3, d2 = lax.optimization_barrier((prompt, d1, d3, d2))
    d2 = y_shift(d2, 2)
    prompt = lax.fori_loop(0, once, lambda i, terms: over_responses(terms), prompt)
    prompt = prompt.reshape(2, NY, PROMPT_ROWS, HD).transpose(1, 0, 2, 3)
    pieces = settle(info, terms, prompt)
    d2, *pieces = lax.optimization_barrier((d2, *pieces))
    attention_out, query_grad, done = lay_rows(info, (d0, d1, d2, d3))
    key_own, value_own, prompt_key_grad, prompt_value_grad = place(
        info, done, by_y(pieces)
    )
    return (
        attention_out[None],
        query_grad[None],
        key_own[None],
        value_own[None],
        prompt_key_grad,
        prompt_value_grad,
    )


def solution(mesh):
    return jax.shard_map(
        per_device,
        mesh=mesh,
        in_specs=(
            P("resp", "prefix", None),
            P("resp", "prefix", None),
            P("resp", "prefix", None),
            P("prefix", None),
            P("prefix", None),
            P("resp", "prefix", None),
            P(),
        ),
        out_specs=(
            P("resp", "prefix", None),
            P("resp", "prefix", None),
            P("resp", "prefix", None),
            P("resp", "prefix", None),
            P("prefix", None),
            P("prefix", None),
        ),
        check_vma=False,
    )
```
